512 devices in a mesh: gx: 32 (over z, core), gy: 16 (over x, y).
Axes of the slice: x: 4, y: 4, z: 16, core: 2. Of those that a mesh axis runs over, the one named last changes fastest.
Arguments:
- points: bfloat16 [262144, 128], P(('gx', 'gy')), may hold values from -6 to 6
- cotangent: bfloat16 [262144, 128], P(('gx', 'gy')), may hold values from -6 to 6
- local_tiles: bfloat16 [262144, 384], P(('gx', 'gy')), may hold values from -0.25 to 0.25
- local_source: int32 [2048, 3], P(('gx', 'gy')), may hold values from 0 to 3
- halo_tiles: bfloat16 [524288, 128], P(('gx', 'gy')), may hold values from -0.25 to 0.25
- cluster_fine: int32 [262144], P(('gx', 'gy')), may hold values from 0 to 511
- cluster_mid: int32 [262144], P(('gx', 'gy')), may hold values from 0 to 511
- cluster_coarse: int32 [262144], P(('gx', 'gy')), may hold values from 0 to 63
- near_weight: bfloat16 [128, 128], replicated, may hold values from -0.5 to 0.5
- up_weights: bfloat16 [3, 128, 128], replicated, may hold values from -0.5 to 0.5
- down_weights: bfloat16 [3, 128, 128], replicated, may hold values from -0.5 to 0.5
Outputs:
- mixed: bfloat16 [262144, 128], P(('gx', 'gy'))
- point_grad: bfloat16 [262144, 128], P(('gx', 'gy'))
- weight_grads: float32 [7, 128, 128], replicated
The draws below stay inside these ranges and needn't reach their ends.
All inputs are finite; a program needn't handle non-finite values.
Results may differ from the reference program's by a relative error of at most 0.018.
Values may be sent and summed in bfloat16 or wider, within the bound.
A program may use at most 64 MiB of HBM per device.

```python
import math
import jax
import jax.numpy as jnp
from jax import lax

C = 128
BLK = 128
KL = 3
LEVELS = 3
C0_DEV = 32
PTS_DEV = 512
NPTS = 262144
BLOCKS = 4
K0 = 512
K1 = 512
K2 = 64
N_GX = 32
N_GY = 16
DEVICES = 512


def mixed_clusters(key, nearby_fn, cluster_count):
    near_key, far_key, chooser_key = jax.random.split(key, 3)
    point_index = jnp.arange(NPTS, dtype=jnp.int32)
    device_index = point_index // PTS_DEV
    nearby = nearby_fn(device_index, near_key) % cluster_count
    anywhere = jax.random.randint(far_key, (NPTS,), 0, cluster_count)
    chooser = jax.random.randint(chooser_key, (NPTS,), 0, 4)
    return jnp.where(chooser == 0, anywhere, nearby).astype(jnp.int32)


def draw_cluster_fine(key, part):
    key = jax.random.fold_in(key, 21)

    def nearby_fn(device_index, near_key):
        column = device_index % N_GY
        return column * C0_DEV + jax.random.randint(near_key, (NPTS,), 0, 2 * C0_DEV)
    return mixed_clusters(key, nearby_fn, K0)


def draw_cluster_mid(key, part):
    key = jax.random.fold_in(key, 22)

    def nearby_fn(device_index, near_key):
        return device_index + jax.random.randint(near_key, (NPTS,), 0, 2)
    return mixed_clusters(key, nearby_fn, K1)


def draw_cluster_coarse(key, part):
    key = jax.random.fold_in(key, 23)

    def nearby_fn(device_index, near_key):
        return device_index // 8 + jax.random.randint(near_key, (NPTS,), 0, 2)
    return mixed_clusters(key, nearby_fn, K2)


def with_ends(result, own_key, smallest, top_value):
    shape = result.shape
    place = [jax.random.randint(jax.random.fold_in(own_key, axis), (), 0, shape[axis]) for axis in range(len(shape))]
    result = result.at[tuple(place)].set(smallest)
    longest = shape.index(max(shape))
    place[longest] = (place[longest] + 1) % shape[longest]
    return result.at[tuple(place)].set(top_value)


def steps_of(stream_key, extent, cuts, smallest, top_value):
    loudness, own = 1.0, jax.random.fold_in(stream_key, 6)
    for position, parts in cuts:
        heights = jnp.exp(jax.random.uniform(jax.random.fold_in(own, position), (parts,), jnp.float32, smallest / len(cuts), top_value / len(cuts)))
        loudness = loudness * jnp.repeat(heights, extent[position] // parts).reshape([-1 if axis == position else 1 for axis in range(len(extent))])
    return loudness


def centred(rng, extent, deviation, most, cuts=(), held_as=jnp.bfloat16):
    drawn = jax.random.normal(rng, extent, jnp.float32) * deviation
    if len(cuts) > 0:
        drawn = steps_of(rng, extent, cuts, -0.22, 0.18) * drawn
    return jnp.clip(drawn, min=-most, max=most).astype(held_as)


def setup_inputs(seed: int = 0) -> dict:
    streams_of = jax.random.split(jax.random.key(seed), 12)
    points = centred(streams_of[0], (NPTS, C), 1.0, 6.0, ((0, 512),))
    cotangent = centred(streams_of[1], (NPTS, C), 1.0, 6.0, ((0, 512),))
    local_tiles = centred(streams_of[2], (NPTS, KL * BLK), (BLK * (KL + 2)) ** -0.5, 0.25, ((0, 512),))
    local_source = with_ends(jax.random.randint(streams_of[3], (NPTS // BLK, KL), 0, BLOCKS), jax.random.fold_in(streams_of[3], 1), 0, BLOCKS - 1).astype(jnp.int32)
    halo_tiles = centred(streams_of[4], (DEVICES * 8 * BLK, BLK), (BLK * (KL + 2)) ** -0.5, 0.25, ((0, 512),))
    cluster_fine = draw_cluster_fine(jax.random.fold_in(streams_of[11], 71), 0)
    cluster_mid = draw_cluster_mid(jax.random.fold_in(streams_of[11], 71), 0)
    cluster_coarse = draw_cluster_coarse(jax.random.fold_in(streams_of[11], 71), 0)
    near_weight = centred(streams_of[8], (C, C), C ** -0.5, 0.5)
    up_weights = centred(streams_of[9], (LEVELS, C, C), C ** -0.5, 0.5)
    down_weights = centred(streams_of[10], (LEVELS, C, C), C ** -0.5, 0.5)
    return {"points": points, "cotangent": cotangent, "local_tiles": local_tiles, "local_source": local_source, "halo_tiles": halo_tiles, "cluster_fine": cluster_fine, "cluster_mid": cluster_mid, "cluster_coarse": cluster_coarse, "near_weight": near_weight, "up_weights": up_weights, "down_weights": down_weights}


EPSILON = 1e-05

def beside_all(corners):
    rest = [(0, 0)] * 4
    padded_x = jnp.pad(corners, [(1, 1), (0, 0)] + rest)
    from_x = jnp.stack([padded_x[:-2, :, 1], padded_x[2:, :, 0]], axis=2)
    padded_y = jnp.pad(corners, [(0, 0), (1, 1)] + rest)
    from_y = jnp.stack([padded_y[:, :-2, :, 1], padded_y[:, 2:, :, 0]], axis=3)
    return (from_x, from_y)

def near_forward(inputs_one):
    device_points, tile_rows, source_index, from_x, from_y, halo_grid = inputs_one
    blocked = device_points.reshape(BLOCKS, BLK, C).astype(jnp.float32)
    sources = blocked[source_index]
    local_grid = tile_rows.reshape(BLOCKS, BLK, KL, BLK).astype(jnp.float32)
    near_field = jnp.einsum('bikj,bkjc->bic', local_grid, sources)
    halo_float = halo_grid.astype(jnp.float32)
    edge_term = jnp.einsum('ijts,ijsc->ijtc', halo_float[:, :, 0], from_x.astype(jnp.float32))
    edge_term = edge_term + jnp.einsum('ijts,ijsc->ijtc', halo_float[:, :, 1], from_y.astype(jnp.float32))
    near_field = jnp.concatenate([near_field[:4] + edge_term.reshape(4, BLK, C), near_field[4:]], axis=0)
    return near_field.reshape(PTS_DEV, C)

def near_backward(inputs_one):
    device_grad, tile_rows, source_index, halo_grid = inputs_one
    blocked_grad = device_grad.reshape(BLOCKS, BLK, C).astype(jnp.float32)
    local_grid = tile_rows.reshape(BLOCKS, BLK, KL, BLK).astype(jnp.float32)
    pieces = jnp.einsum('bikj,bic->bkjc', local_grid, blocked_grad)
    returned = jax.ops.segment_sum(pieces.reshape(BLOCKS * KL, BLK, C), source_index.reshape(-1), num_segments=BLOCKS)
    corner_grad = blocked_grad[:4].reshape(2, 2, BLK, C)
    halo_float = halo_grid.astype(jnp.float32)
    push_x = jnp.einsum('ijts,ijtc->ijsc', halo_float[:, :, 0], corner_grad)
    push_y = jnp.einsum('ijts,ijtc->ijsc', halo_float[:, :, 1], corner_grad)
    return (returned, push_x, push_y)

def reference(points, cotangent, local_tiles, local_source, halo_tiles, cluster_fine, cluster_mid, cluster_coarse, near_weight, up_weights, down_weights):
    devices_all = N_GX * N_GY
    corners = points.reshape(N_GX, N_GY, BLOCKS, BLK, C)[:, :, :4].reshape(N_GX, N_GY, 2, 2, BLK, C)
    from_x, from_y = beside_all(corners)
    halo_grid = halo_tiles.reshape(devices_all, 2, 2, 2, BLK, BLK)
    tile_rows = local_tiles.reshape(devices_all, PTS_DEV, KL * BLK)
    source_index = local_source.reshape(devices_all, BLOCKS, KL)
    near_field = lax.map(near_forward, (points.reshape(devices_all, PTS_DEV, C), tile_rows, source_index, from_x.reshape(devices_all, 2, 2, BLK, C), from_y.reshape(devices_all, 2, 2, BLK, C), halo_grid))
    near_values = near_field.reshape(NPTS, C).astype(jnp.bfloat16)
    point_index = jnp.arange(NPTS, dtype=jnp.int32)
    row_group = point_index // (PTS_DEV * N_GY)
    segments = [(row_group * K0 + cluster_fine, N_GX * K0), (cluster_mid, K1), (cluster_coarse, K2)]
    level_input = points
    inputs_list = []
    normed_list = []
    inverse_list = []
    gathered_list = []
    for level_index in range(LEVELS):
        segment_ids, segment_count = segments[level_index]
        up_values = jnp.dot(level_input, up_weights[level_index], preferred_element_type=jnp.float32).astype(jnp.bfloat16)
        summed = jax.ops.segment_sum(up_values.astype(jnp.float32), segment_ids, num_segments=segment_count)
        inverse_rms = lax.rsqrt(lax.optimization_barrier(jnp.mean(summed * summed, axis=-1, keepdims=True)) + EPSILON)
        normed = summed * inverse_rms
        gathered = normed[segment_ids].astype(jnp.bfloat16)
        inputs_list.append(level_input)
        normed_list.append(normed)
        inverse_list.append(inverse_rms)
        gathered_list.append(gathered)
        level_input = gathered
    combined = points.astype(jnp.float32) + jnp.dot(near_values, near_weight, preferred_element_type=jnp.float32)
    for level_index in range(LEVELS):
        combined = combined + jnp.dot(gathered_list[level_index], down_weights[level_index], preferred_element_type=jnp.float32)
    mixed = combined.astype(jnp.bfloat16)
    near_grad = jnp.dot(cotangent, near_weight.T, preferred_element_type=jnp.float32).astype(jnp.bfloat16)
    up_grads = [None] * LEVELS
    down_grads = [None] * LEVELS
    upper = None
    for level_index in range(LEVELS - 1, -1, -1):
        segment_ids, segment_count = segments[level_index]
        level_grad = jnp.dot(cotangent, down_weights[level_index].T, preferred_element_type=jnp.float32)
        if upper is not None:
            level_grad = level_grad + jnp.dot(upper, up_weights[level_index + 1].T, preferred_element_type=jnp.float32)
        level_grad = level_grad.astype(jnp.bfloat16)
        summed_grad = jax.ops.segment_sum(level_grad.astype(jnp.float32), segment_ids, num_segments=segment_count)
        normed = normed_list[level_index]
        summed_grad = inverse_list[level_index] * (summed_grad - normed * lax.optimization_barrier(jnp.mean(summed_grad * normed, axis=-1, keepdims=True)))
        upper = summed_grad[segment_ids].astype(jnp.bfloat16)
        up_grads[level_index] = jnp.dot(inputs_list[level_index].T, upper, preferred_element_type=jnp.float32)
        down_grads[level_index] = jnp.dot(gathered_list[level_index].T, cotangent, preferred_element_type=jnp.float32)
    returned, push_x, push_y = lax.map(near_backward, (near_grad.reshape(devices_all, PTS_DEV, C), tile_rows, source_index, halo_grid))
    return_x = beside_all(push_x.reshape(N_GX, N_GY, 2, 2, BLK, C))[0]
    return_y = beside_all(push_y.reshape(N_GX, N_GY, 2, 2, BLK, C))[1]
    edge_back = (return_x + return_y).reshape(devices_all, 4, BLK, C)
    returned = jnp.concatenate([returned[:, :4] + edge_back, returned[:, 4:]], axis=1)
    point_grad = (cotangent.astype(jnp.float32) + returned.reshape(NPTS, C) + jnp.dot(upper, up_weights[0].T, preferred_element_type=jnp.float32)).astype(jnp.bfloat16)
    grad_list = [jnp.dot(near_values.T, cotangent, preferred_element_type=jnp.float32)] + up_grads + down_grads
    weight_grads = jnp.stack(grad_list) * (1.0 / math.sqrt(NPTS))
    return (mixed, point_grad, weight_grads)
```

```python
import functools
import math

import jax
import jax.numpy as jnp
from jax import lax
from jax.experimental import pallas as pl
from jax.experimental.pallas import tpu as pltpu
from jax.sharding import PartitionSpec as P

BLK = 128
C = 128
PTS = 512
OWN0 = 32
EPSILON = 1e-05
MESH = pl.DeviceIdType.MESH
F32, BF16 = jnp.float32, jnp.bfloat16

NN = ((1,), (0,))
NT = ((1,), (1,))
TN = ((0,), (0,))


def dot(a, b, dims=NN):
    return lax.dot_general(a, b, (dims, ((), ())), preferred_element_type=F32)


def dot_split(a, b, dims=NN):
    high = a.astype(BF16)
    low = (a - high.astype(F32)).astype(BF16)
    return dot(high, b, dims) + dot(low, b, dims)


def one_hot_rows(ids, first, count):
    rows = lax.broadcasted_iota(jnp.int32, (count, ids.shape[1]), 0) + first
    return jnp.where(rows == ids, 1.0, 0.0).astype(BF16)


def inverse_rms(summed):
    return lax.rsqrt(jnp.mean(summed * summed, axis=-1, keepdims=True) + EPSILON)


def norm_back(raw, normed, inverse):
    return inverse * (raw - normed * jnp.mean(raw * normed, axis=-1, keepdims=True))


def kernel(
    size_x,
    size_y,
    pts_ref,
    cot_ref,
    tiles_ref,
    src_ref,
    halo_ref,
    c0_ref,
    c1_ref,
    c2_ref,
    nw_ref,
    up_ref,
    dn_ref,
    mixed_ref,
    pg_ref,
    wg_ref,
    ot0,
    ot1,
    ot2,
    near,
    ret,
    nv,
    spx,
    spy,
    fx,
    fy,
    bx,
    by,
    ids,
    s_u0,
    r_u0,
    s_t0,
    r_t0,
    s_p1,
    r_p1,
    z_p1,
    p1,
    s_u1,
    r_u1,
    z_u1,
    u1,
    n0all,
    sg0all,
    s_p2,
    r_p2,
    z_p2,
    g_p2,
    s_d,
    r_d,
    z_d,
    g_d,
    send_sem,
    recv_sem,
    halo_send,
    halo_recv,
):
    size_z = size_x // 2
    size_q = 2 * size_y
    k1 = size_x * size_y
    k2 = k1 // 8
    a = lax.axis_index("gx")
    b = lax.axis_index("gy")
    z = lax.div(a, 2)
    core = lax.rem(a, 2)
    q = core * size_y + b
    scale = 1.0 / math.sqrt(PTS * size_x * size_y)

    def peer(kind, o):
        if kind == "y":
            i = lax.rem(b + o, size_y)
            return i, (a, i)
        if kind == "z":
            i = lax.rem(z + o, size_z)
            return i, (i * 2 + core, b)
        i = lax.rem(q + o, size_q)
        return i, (z * 2 + lax.div(i, size_y), lax.rem(i, size_y))

    count = {"y": size_y, "z": size_z, "q": size_q}

    def exchange(kind, step, source, target):
        def body(o, carry):
            i, device = peer(kind, o)
            pltpu.make_async_remote_copy(
                src_ref=source(i),
                dst_ref=target,
                send_sem=send_sem.at[step],
                recv_sem=recv_sem.at[step],
                device_id=device,
                device_id_type=MESH,
            ).start()
            return carry

        lax.fori_loop(1, count[kind], body, 0)

    def arrived(step, ref):
        pltpu.make_async_copy(ref, ref, recv_sem.at[step]).wait()

    def sent(step, ref):
        pltpu.make_async_copy(ref, ref, send_sem.at[step]).wait()

    barrier = pltpu.get_barrier_semaphore()

    def greet(kind):
        def body(o, carry):
            _, device = peer(kind, o)
            pl.semaphore_signal(barrier, inc=1, device_id=device, device_id_type=MESH)
            return carry

        lax.fori_loop(1, count[kind], body, 0)

    greet("z")
    greet("q")
    beside = lax.rem(a + size_x - 1 + 2 * core, size_x)
    pl.semaphore_signal(barrier, inc=1, device_id=(beside, b), device_id_type=MESH)

    points = pts_ref[...].reshape(PTS, C)
    cot = cot_ref[...]
    c0, c1, c2 = c0_ref[...], c1_ref[...], c2_ref[...]
    ot0[...] = one_hot_rows(c0, 0, OWN0 * size_y)
    ot1[...] = one_hot_rows(c1, 0, k1)
    ot2[...] = one_hot_rows(c2, 0, C)
    both = dot(ot0[...], jnp.concatenate([points, cot], axis=1))
    s_u0[...] = both[:, :C].astype(BF16)
    s_t0[...] = both[:, C:].astype(BF16)
    ids[b] = c0 * 1024 + c1
    lane = lax.broadcasted_iota(jnp.int32, (k2, C), 1)
    t2 = dot(ot2[...], cot)[:k2]
    s_p1[:, :C] = dot(ot1[...], cot).astype(BF16)
    counts = dot(ot1[...], ot2[...], NT)
    s_p1[2 * k2 :, C:] = counts[2 * k2 :].astype(BF16)
    s_p1[:k2, C:] = jnp.where(lane < k2, counts[:k2], pltpu.roll(t2, C - k2, 1)).astype(BF16)
    s_p1[k2 : 2 * k2, C:] = jnp.where(lane < k2, counts[k2 : 2 * k2], t2).astype(BF16)

    near_grad = dot(cot, nw_ref[...], NT).astype(BF16)
    returned = [jnp.zeros((BLK, C), F32)] * 4
    for t in range(4):
        rows = slice(t * BLK, (t + 1) * BLK)
        tile = tiles_ref[rows, :]
        sources = jnp.concatenate([pts_ref[src_ref[t, k]] for k in range(3)], axis=0)
        near[t] = dot(tile, sources)
        grad = near_grad[rows]
        pieces = dot(tile, grad, TN)
        for k in range(3):
            piece = pieces[k * BLK : (k + 1) * BLK]
            for s in range(4):
                returned[s] = returned[s] + jnp.where(src_ref[t, k] == s, piece, 0.0)
        spx[t] = dot(halo_ref[2 * t], grad, TN).astype(BF16)
        spy[t] = dot(halo_ref[2 * t + 1], grad, TN).astype(BF16)
    for s in range(4):
        ret[s] = returned[s]

    pl.semaphore_wait(barrier, size_z - 1 + size_q - 1 + 1)

    exchange("y", 0, lambda i: ids.at[b], ids.at[b])
    exchange("y", 1, lambda i: s_u0.at[pl.ds(i * OWN0, OWN0)], r_u0.at[b])
    exchange("q", 2, lambda i: s_p1.at[pl.ds(i * 16, 16)], r_p1.at[q])
    exchange("y", 3, lambda i: s_t0.at[pl.ds(i * OWN0, OWN0)], r_t0.at[b])
    has = (a > 0, a < size_x - 1, b > 0, b < size_y - 1)

    def halo_copies(side):
        if side == 0:
            return [[(pts_ref.at[pl.ds(0, 2)], fx.at[pl.ds(2, 2)])], [(spx.at[pl.ds(0, 2)], bx.at[pl.ds(2, 2)])]]
        if side == 1:
            return [[(pts_ref.at[pl.ds(2, 2)], fx.at[pl.ds(0, 2)])], [(spx.at[pl.ds(2, 2)], bx.at[pl.ds(0, 2)])]]
        if side == 2:
            return [[(pts_ref.at[i], fy.at[i + 1]) for i in (0, 2)], [(spy.at[i], by.at[i + 1]) for i in (0, 2)]]
        return [[(pts_ref.at[i], fy.at[i - 1]) for i in (1, 3)], [(spy.at[i], by.at[i - 1]) for i in (1, 3)]]

    neighbour = ((a - 1, b), (a + 1, b), (a, b - 1), (a, b + 1))
    for side in range(4):

        @pl.when(has[side])
        def _(side=side):
            for kind in range(2):
                for source, target in halo_copies(side)[kind]:
                    pltpu.make_async_remote_copy(
                        src_ref=source,
                        dst_ref=target,
                        send_sem=halo_send.at[2 * side + kind],
                        recv_sem=halo_recv.at[2 * (side ^ 1) + kind],
                        device_id=neighbour[side],
                        device_id_type=MESH,
                    ).start()

    arrived(0, ids.at[pl.ds(0, size_y - 1)])
    pair_counts = jnp.zeros((OWN0, k1), F32)
    for i in range(size_y):
        packed = ids[i]
        fine = lax.shift_right_logical(packed, 10)
        mid = lax.bitwise_and(packed, 1023)
        pair_counts = pair_counts + dot(
            one_hot_rows(fine, b * OWN0, OWN0), one_hot_rows(mid, 0, k1), NT
        )
    pair_counts = pair_counts.astype(BF16)

    r_u0[b] = s_u0[pl.ds(pl.multiple_of(b * OWN0, OWN0), OWN0), :]
    arrived(1, r_u0.at[pl.ds(0, size_y - 1)])
    u0 = jnp.sum(r_u0[...].astype(F32), axis=0)
    summed0 = dot_split(u0, up_ref[0])
    inverse0 = inverse_rms(summed0)
    normed0 = summed0 * inverse0
    n0 = normed0.astype(BF16)
    s_u1[...] = dot(pair_counts, n0, TN).astype(BF16)
    exchange("q", 4, lambda i: s_u1.at[pl.ds(i * 16, 16)], r_u1.at[q])
    mine32 = pl.ds(pl.multiple_of(b * OWN0, OWN0), OWN0)
    n0all[mine32, :] = n0
    exchange("y", 5, lambda i: n0all.at[mine32], n0all.at[mine32])

    mine16 = pl.ds(pl.multiple_of(q * 16, 16), 16)
    r_p1[q] = s_p1[mine16, :]
    arrived(2, r_p1.at[pl.ds(0, size_q - 1)])
    z_p1[z] = jnp.sum(r_p1[...].astype(F32), axis=0).astype(BF16)
    exchange("z", 6, lambda i: z_p1.at[z], z_p1.at[z])

    r_t0[b] = s_t0[mine32, :]
    arrived(3, r_t0.at[pl.ds(0, size_y - 1)])
    t0 = jnp.sum(r_t0[...].astype(F32), axis=0)

    for side in range(4):
        got = (
            (fx.at[pl.ds(0, 2)], bx.at[pl.ds(0, 2)])
            if side == 0
            else (fx.at[pl.ds(2, 2)], bx.at[pl.ds(2, 2)])
            if side == 1
            else (fy.at[pl.ds(0, 2)], by.at[pl.ds(0, 2)])
        )

        @pl.when(has[side])
        def _(side=side, got=got):
            for kind in range(2):
                pltpu.make_async_copy(got[kind], got[kind], halo_recv.at[2 * side + kind]).wait()

        @pl.when(jnp.logical_not(has[side]))
        def _(side=side):
            for i in ((0, 1), (2, 3), (0, 2), (1, 3))[side]:
                for ref in ((fx, bx) if side < 2 else (fy, by)):
                    ref[i] = jnp.zeros((BLK, C), BF16)

    for t in range(4):
        total = near[t] + dot(halo_ref[2 * t], fx[t]) + dot(halo_ref[2 * t + 1], fy[t])
        nv[pl.ds(t * BLK, BLK), :] = total.astype(BF16)
        ret[t] = ret[t] + bx[t].astype(F32) + by[t].astype(F32)
    near_part = dot(nv[...], cot, TN)
    down0_part = dot(n0, t0.astype(BF16), TN)
    s_p2[...] = jnp.concatenate(
        [near_part.reshape(size_y, 8, C), down0_part.reshape(size_y, 8, C)], axis=1
    ).astype(BF16)
    exchange("q", 7, lambda i: s_p2.at[lax.rem(i, size_y)], r_p2.at[q])

    r_u1[q] = s_u1[mine16, :]
    arrived(4, r_u1.at[pl.ds(0, size_q - 1)])
    z_u1[z] = jnp.sum(r_u1[...].astype(F32), axis=0).astype(BF16)
    exchange("z", 8, lambda i: z_u1.at[z], z_u1.at[z])

    arrived(6, z_p1.at[pl.ds(0, size_z - 1)])
    p1[mine16, :] = jnp.sum(z_p1[...].astype(F32), axis=0).astype(BF16)
    exchange("q", 9, lambda i: p1.at[mine16], p1.at[mine16])

    r_p2[q] = s_p2[b]
    arrived(7, r_p2.at[pl.ds(0, size_q - 1)])
    z_p2[z] = jnp.sum(r_p2[...].astype(F32), axis=0).astype(BF16)
    exchange("z", 10, lambda i: z_p2.at[z], z_p2.at[z])

    arrived(8, z_u1.at[pl.ds(0, size_z - 1)])
    u1[mine16, :] = jnp.sum(z_u1[...].astype(F32), axis=0).astype(BF16)
    exchange("q", 11, lambda i: u1.at[mine16], u1.at[mine16])

    arrived(10, z_p2.at[pl.ds(0, size_z - 1)])
    g_p2[b] = jnp.sum(z_p2[...].astype(F32), axis=0) * scale
    exchange("y", 12, lambda i: g_p2.at[b], g_p2.at[b])

    arrived(9, p1.at[pl.ds(0, (size_q - 1) * 16)])
    t1 = p1[:, :C]
    upper_part = p1[:k2, C:].astype(F32)
    t2 = jnp.where(lane < k2, pltpu.roll(upper_part, C - k2, 1), p1[k2 : 2 * k2, C:].astype(F32))
    t2 = t2.astype(BF16)
    counts = p1[:, C:][:, :k2]

    raw2 = dot(t2, dn_ref[2], NT)
    raw1 = dot(t1, dn_ref[1], NT)
    raw0 = dot_split(t0, dn_ref[0], NT)
    arrived(11, u1.at[pl.ds(0, (size_q - 1) * 16)])
    summed1 = dot(u1[...], up_ref[1])
    inverse1 = inverse_rms(summed1)
    normed1 = summed1 * inverse1
    n1 = normed1.astype(BF16)
    u2 = dot(counts, n1, TN)
    summed2 = dot_split(u2, up_ref[2])
    inverse2 = inverse_rms(summed2)
    normed2 = summed2 * inverse2
    n2 = normed2.astype(BF16)
    sg2 = norm_back(raw2, normed2, inverse2).astype(BF16)
    raw1 = raw1 + dot_split(dot(counts, sg2), up_ref[2], NT)
    sg1 = norm_back(raw1, normed1, inverse1).astype(BF16)
    raw0 = raw0 + dot_split(dot(pair_counts, sg1), up_ref[1], NT)
    sg0 = norm_back(raw0, normed0, inverse0).astype(BF16)
    s_d[...] = dot_split(u0, sg0, TN).reshape(size_y, 8, C)
    exchange("q", 13, lambda i: s_d.at[lax.rem(i, size_y)], r_d.at[q])
    sg0all[mine32, :] = sg0
    exchange("y", 14, lambda i: sg0all.at[mine32], sg0all.at[mine32])

    wg_ref[2] = dot(u1[...], sg1, TN) * scale
    wg_ref[3] = dot_split(u2, sg2, TN) * scale
    wg_ref[5] = dot(n1, t1, TN) * scale
    wg_ref[6] = dot(n2, t2, TN) * scale

    arrived(5, n0all.at[pl.ds(0, (size_y - 1) * OWN0)])
    combined = points.astype(F32) + dot(nv[...], nw_ref[...])
    combined = combined + dot(dot(ot0[...], n0all[...], TN).astype(BF16), dn_ref[0])
    combined = combined + dot(dot(ot1[...], n1, TN).astype(BF16), dn_ref[1])
    combined = combined + dot(dot(ot2[:k2, :], n2, TN).astype(BF16), dn_ref[2])
    mixed_ref[...] = combined.astype(BF16)

    r_d[q] = s_d[b]
    arrived(13, r_d.at[pl.ds(0, size_q - 1)])
    z_d[z] = jnp.sum(r_d[...], axis=0)
    exchange("z", 15, lambda i: z_d.at[z], z_d.at[z])

    arrived(14, sg0all.at[pl.ds(0, (size_y - 1) * OWN0)])
    upper0 = dot(ot0[...], sg0all[...], TN).astype(BF16)
    grad = cot.astype(F32) + ret[...].reshape(PTS, C) + dot(upper0, up_ref[0], NT)
    pg_ref[...] = grad.astype(BF16)

    arrived(12, g_p2.at[pl.ds(0, size_y - 1)])
    wg_ref[0] = g_p2[:, :8, :].reshape(C, C)
    wg_ref[4] = g_p2[:, 8:, :].reshape(C, C)

    arrived(15, z_d.at[pl.ds(0, size_z - 1)])
    g_d[b] = jnp.sum(z_d[...], axis=0) * scale
    exchange("y", 16, lambda i: g_d.at[b], g_d.at[b])
    for step, ref in (
        (0, ids.at[pl.ds(0, size_y - 1)]),
        (1, r_u0.at[pl.ds(0, size_y - 1)]),
        (2, r_p1.at[pl.ds(0, size_q - 1)]),
        (3, r_t0.at[pl.ds(0, size_y - 1)]),
        (4, r_u1.at[pl.ds(0, size_q - 1)]),
        (5, n0all.at[pl.ds(0, (size_y - 1) * OWN0)]),
        (6, z_p1.at[pl.ds(0, size_z - 1)]),
        (7, r_p2.at[pl.ds(0, size_q - 1)]),
        (8, z_u1.at[pl.ds(0, size_z - 1)]),
        (9, p1.at[pl.ds(0, (size_q - 1) * 16)]),
        (10, z_p2.at[pl.ds(0, size_z - 1)]),
        (11, u1.at[pl.ds(0, (size_q - 1) * 16)]),
        (12, g_p2.at[pl.ds(0, size_y - 1)]),
        (13, r_d.at[pl.ds(0, size_q - 1)]),
        (14, sg0all.at[pl.ds(0, (size_y - 1) * OWN0)]),
        (15, z_d.at[pl.ds(0, size_z - 1)]),
    ):
        sent(step, ref)
    for side in range(4):

        @pl.when(has[side])
        def _(side=side):
            for kind in range(2):
                two = fx.at[pl.ds(0, 2)]
                pltpu.make_async_copy(two, two, halo_send.at[2 * side + kind]).wait()

    arrived(16, g_d.at[pl.ds(0, size_y - 1)])
    sent(16, g_d.at[pl.ds(0, size_y - 1)])
    wg_ref[1] = g_d[...].reshape(C, C)


def on_device(
    size_x,
    size_y,
    points,
    cotangent,
    local_tiles,
    local_source,
    halo_tiles,
    cluster_fine,
    cluster_mid,
    cluster_coarse,
    near_weight,
    up_weights,
    down_weights,
):
    size_z, size_q, k1 = size_x // 2, 2 * size_y, size_x * size_y
    vmem = pl.BlockSpec(memory_space=pltpu.VMEM)
    smem = pl.BlockSpec(memory_space=pltpu.SMEM)
    k0 = OWN0 * size_y
    blocks = pltpu.VMEM((4, BLK, C), BF16)
    scratch = [
        pltpu.VMEM((k0, PTS), BF16),
        pltpu.VMEM((k1, PTS), BF16),
        pltpu.VMEM((C, PTS), BF16),
        pltpu.VMEM((4, BLK, C), F32),
        pltpu.VMEM((4, BLK, C), F32),
        pltpu.VMEM((PTS, C), BF16),
        blocks,
        blocks,
        blocks,
        blocks,
        blocks,
        blocks,
        pltpu.VMEM((size_y, 1, PTS), jnp.int32),
        pltpu.VMEM((k0, C), BF16),
        pltpu.VMEM((size_y, OWN0, C), BF16),
        pltpu.VMEM((k0, C), BF16),
        pltpu.VMEM((size_y, OWN0, C), BF16),
        pltpu.VMEM((k1, 2 * C), BF16),
        pltpu.VMEM((size_q, 16, 2 * C), BF16),
        pltpu.VMEM((size_z, 16, 2 * C), BF16),
        pltpu.VMEM((k1, 2 * C), BF16),
        pltpu.VMEM((k1, C), BF16),
        pltpu.VMEM((size_q, 16, C), BF16),
        pltpu.VMEM((size_z, 16, C), BF16),
        pltpu.VMEM((k1, C), BF16),
        pltpu.VMEM((k0, C), BF16),
        pltpu.VMEM((k0, C), BF16),
        pltpu.VMEM((size_y, 16, C), BF16),
        pltpu.VMEM((size_q, 16, C), BF16),
        pltpu.VMEM((size_z, 16, C), BF16),
        pltpu.VMEM((size_y, 16, C), F32),
        pltpu.VMEM((size_y, 8, C), F32),
        pltpu.VMEM((size_q, 8, C), F32),
        pltpu.VMEM((size_z, 8, C), F32),
        pltpu.VMEM((size_y, 8, C), F32),
        pltpu.SemaphoreType.DMA((17,)),
        pltpu.SemaphoreType.DMA((17,)),
        pltpu.SemaphoreType.DMA((8,)),
        pltpu.SemaphoreType.DMA((8,)),
    ]
    return pl.pallas_call(
        functools.partial(kernel, size_x, size_y),
        out_shape=(
            jax.ShapeDtypeStruct((PTS, C), BF16),
            jax.ShapeDtypeStruct((PTS, C), BF16),
            jax.ShapeDtypeStruct((7, C, C), F32),
        ),
        in_specs=[vmem, vmem, vmem, smem, vmem, vmem, vmem, vmem, vmem, vmem, vmem],
        out_specs=(vmem, vmem, vmem),
        scratch_shapes=scratch,
        name="layer",
        compiler_params=pltpu.CompilerParams(
            collective_id=0, has_side_effects=True, vmem_limit_bytes=48 * 1024 * 1024
        ),
    )(
        points.reshape(4, BLK, C),
        cotangent,
        local_tiles,
        local_source,
        halo_tiles.reshape(8, BLK, BLK),
        cluster_fine.reshape(1, PTS),
        cluster_mid.reshape(1, PTS),
        cluster_coarse.reshape(1, PTS),
        near_weight,
        up_weights,
        down_weights,
    )


def solution(mesh):
    rows = P(("gx", "gy"), None)
    flat = P(("gx", "gy"))
    size_x, size_y = mesh.shape["gx"], mesh.shape["gy"]
    return jax.shard_map(
        functools.partial(on_device, size_x, size_y),
        mesh=mesh,
        in_specs=(rows, rows, rows, rows, rows, flat, flat, flat, P(), P(), P()),
        out_specs=(rows, rows, P()),
        check_vma=False,
    )
```

```python
import functools
import math

import jax
import jax.numpy as jnp
from jax import lax
from jax.experimental import pallas as pl
from jax.experimental.pallas import tpu as pltpu
from jax.sharding import PartitionSpec as P

BLK = 128
C = 128
PTS = 512
OWN0 = 32
EPSILON = 1e-05
MESH = pl.DeviceIdType.MESH
F32, BF16 = jnp.float32, jnp.bfloat16

NN = ((1,), (0,))
NT = ((1,), (1,))
TN = ((0,), (0,))


def dot(a, b, dims=NN):
    return lax.dot_general(a, b, (dims, ((), ())), preferred_element_type=F32)


def dot_split(a, b, dims=NN):
    high = a.astype(BF16)
    low = (a - high.astype(F32)).astype(BF16)
    return dot(high, b, dims) + dot(low, b, dims)


def one_hot_rows(ids, first, count):
    rows = lax.broadcasted_iota(jnp.int32, (count, ids.shape[1]), 0) + first
    return jnp.where(rows == ids, 1.0, 0.0).astype(BF16)


def inverse_rms(summed):
    return lax.rsqrt(jnp.mean(summed * summed, axis=-1, keepdims=True) + EPSILON)


def norm_back(raw, normed, inverse):
    return inverse * (raw - normed * jnp.mean(raw * normed, axis=-1, keepdims=True))


def kernel(
    size_x,
    size_y,
    pts_in,
    cot_in,
    tiles_in,
    src_in,
    halo_in,
    c0_in,
    c1_in,
    c2_in,
    nw_in,
    up_in,
    dn_in,
    mixed_out,
    pg_out,
    wg_out,
    mixed_ref,
    pg_ref,
    wg_ref,
    out_sem,
    pts_ref,
    cot_ref,
    tiles_ref,
    src_ref,
    halo_ref,
    c0_ref,
    c1_ref,
    c2_ref,
    nw_ref,
    up_ref,
    dn_ref,
    load_sem,
    ot0,
    ot1,
    ot2,
    near,
    ret,
    nv,
    spx,
    spy,
    fx,
    fy,
    bx,
    by,
    ids,
    s_u0,
    r_u0,
    s_t0,
    r_t0,
    s_p1,
    r_p1,
    z_p1,
    p1,
    s_u1,
    r_u1,
    z_u1,
    u1,
    ut0,
    u0_t,
    cat0,
    cat1,
    group,
    group_bf,
    s_p2,
    r_p2,
    z_p2,
    g_p2,
    s_d,
    r_d,
    z_d,
    g_d,
    send_sem,
    recv_sem,
    halo_send,
    halo_recv,
    ids_recv,
    relay,
):
    size_z = size_x // 2
    size_q = 2 * size_y
    k1 = size_x * size_y
    k2 = k1 // 8
    a = lax.axis_index("gx")
    b = lax.axis_index("gy")
    z = lax.div(a, 2)
    core = lax.rem(a, 2)
    q = core * size_y + b
    scale = 1.0 / math.sqrt(PTS * size_x * size_y)

    def peer(kind, o):
        if kind == "y":
            i = lax.rem(b + o, size_y)
            return i, (a, i)
        if kind == "z":
            i = lax.rem(z + o, size_z)
            return i, (i * 2 + core, b)
        i = lax.rem(q + o, size_q)
        return i, (z * 2 + lax.div(i, size_y), lax.rem(i, size_y))

    count = {"y": size_y, "z": size_z, "q": size_q}

    def exchange(kind, step, source, target, landed=None):
        def body(o, carry):
            i, device = peer(kind, o)
            pltpu.make_async_remote_copy(
                src_ref=source(i),
                dst_ref=target,
                send_sem=send_sem.at[step],
                recv_sem=recv_sem.at[step] if landed is None else landed,
                device_id=device,
                device_id_type=MESH,
            ).start()
            return carry

        lax.fori_loop(1, count[kind], body, 0)

    def arrived(step, ref):
        pltpu.make_async_copy(ref, ref, recv_sem.at[step]).wait()

    def id_arrived(i):
        pltpu.make_async_copy(ids.at[i], ids.at[i], ids_recv.at[i]).wait()

    def sent(step, ref):
        pltpu.make_async_copy(ref, ref, send_sem.at[step]).wait()

    loads = {
        name: pltpu.make_async_copy(source, target, load_sem.at[i])
        for i, (name, source, target) in enumerate(
            (
                ("c0", c0_in, c0_ref),
                ("pts", pts_in, pts_ref),
                ("cot", cot_in, cot_ref),
                ("c1", c1_in, c1_ref),
                ("c2", c2_in, c2_ref),
                ("nw", nw_in, nw_ref),
                ("src", src_in, src_ref),
                ("tiles", tiles_in, tiles_ref),
                ("halo", halo_in, halo_ref),
                ("up", up_in, up_ref),
                ("dn", dn_in, dn_ref),
            )
        )
    }
    for load in loads.values():
        load.start()

    barrier = pltpu.get_barrier_semaphore()

    reach = size_z // 4

    def greet(kind, steps, shift):
        def body(o, carry):
            _, device = peer(kind, o + shift)
            pl.semaphore_signal(barrier, inc=1, device_id=device, device_id_type=MESH)
            return carry

        lax.fori_loop(1, steps + 1, body, 0)

    greet("z", reach, 0)
    greet("z", reach, size_z - reach - 1)
    greet("q", size_q - 1, 0)
    beside = lax.rem(a + size_x - 1 + 2 * core, size_x)
    pl.semaphore_signal(barrier, inc=1, device_id=(beside, b), device_id_type=MESH)

    for name in ("c0", "pts", "cot", "c1", "c2"):
        loads[name].wait()
    points = pts_ref[...].reshape(PTS, C)
    cot = cot_ref[...]
    c0, c1, c2 = c0_ref[...], c1_ref[...], c2_ref[...]
    ot0[...] = one_hot_rows(c0, 0, OWN0 * size_y)
    ot1[...] = one_hot_rows(c1, 0, k1)
    ot2[...] = one_hot_rows(c2, 0, C)
    both = dot(ot0[...], jnp.concatenate([points, cot], axis=1))
    s_u0[...] = both[:, :C].astype(BF16)
    s_t0[...] = both[:, C:].astype(BF16)
    ids[b] = c0 * 1024 + c1
    lane = lax.broadcasted_iota(jnp.int32, (k2, C), 1)
    t2 = dot(ot2[...], cot)[:k2]
    s_p1[:, :C] = dot(ot1[...], cot).astype(BF16)
    counts = dot(ot1[...], ot2[...], NT)
    s_p1[2 * k2 :, C:] = counts[2 * k2 :].astype(BF16)
    s_p1[:k2, C:] = jnp.where(lane < k2, counts[:k2], pltpu.roll(t2, C - k2, 1)).astype(BF16)
    s_p1[k2 : 2 * k2, C:] = jnp.where(lane < k2, counts[k2 : 2 * k2], t2).astype(BF16)

    for name in ("nw", "src", "tiles", "halo", "up", "dn"):
        loads[name].wait()
    near_grad = dot(cot, nw_ref[...], NT).astype(BF16)
    returned = [jnp.zeros((BLK, C), F32)] * 4
    for t in range(4):
        rows = slice(t * BLK, (t + 1) * BLK)
        tile = tiles_ref[rows, :]
        sources = jnp.concatenate([pts_ref[src_ref[t, k]] for k in range(3)], axis=0)
        near[t] = dot(tile, sources)
        grad = near_grad[rows]
        pieces = dot(tile, grad, TN)
        for k in range(3):
            piece = pieces[k * BLK : (k + 1) * BLK]
            for s in range(4):
                returned[s] = returned[s] + jnp.where(src_ref[t, k] == s, piece, 0.0)
        spx[t] = dot(halo_ref[2 * t], grad, TN).astype(BF16)
        spy[t] = dot(halo_ref[2 * t + 1], grad, TN).astype(BF16)
    for s in range(4):
        ret[s] = returned[s]

    pl.semaphore_wait(barrier, 2 * reach + size_q - 1 + 1)
    for o in (reach, size_z - reach):
        _, device = peer("z", o)
        pl.semaphore_signal(relay, inc=1, device_id=device, device_id_type=MESH)

    exchange("y", 0, lambda i: ids.at[b], ids.at[b], ids_recv.at[b])
    exchange("y", 1, lambda i: s_u0.at[pl.ds(i * OWN0, OWN0)], r_u0.at[b])
    exchange("q", 2, lambda i: s_p1.at[pl.ds(i * 16, 16)], r_p1.at[q])
    exchange("y", 3, lambda i: s_t0.at[pl.ds(i * OWN0, OWN0)], r_t0.at[b])
    has = (a > 0, a < size_x - 1, b > 0, b < size_y - 1)

    def halo_copies(side):
        if side == 0:
            return [[(pts_ref.at[pl.ds(0, 2)], fx.at[pl.ds(2, 2)])], [(spx.at[pl.ds(0, 2)], bx.at[pl.ds(2, 2)])]]
        if side == 1:
            return [[(pts_ref.at[pl.ds(2, 2)], fx.at[pl.ds(0, 2)])], [(spx.at[pl.ds(2, 2)], bx.at[pl.ds(0, 2)])]]
        if side == 2:
            return [[(pts_ref.at[i], fy.at[i + 1]) for i in (0, 2)], [(spy.at[i], by.at[i + 1]) for i in (0, 2)]]
        return [[(pts_ref.at[i], fy.at[i - 1]) for i in (1, 3)], [(spy.at[i], by.at[i - 1]) for i in (1, 3)]]

    neighbour = ((a - 1, b), (a + 1, b), (a, b - 1), (a, b + 1))
    for side in range(4):

        @pl.when(has[side])
        def _(side=side):
            for kind in range(2):
                for source, target in halo_copies(side)[kind]:
                    pltpu.make_async_remote_copy(
                        src_ref=source,
                        dst_ref=target,
                        send_sem=halo_send.at[2 * side + kind],
                        recv_sem=halo_recv.at[2 * (side ^ 1) + kind],
                        device_id=neighbour[side],
                        device_id_type=MESH,
                    ).start()

    side_y = math.isqrt(size_y)
    near_first = sorted(
        ((dx, dy) for dx in range(side_y) for dy in range(size_y // side_y)),
        key=lambda d: min(d[0], side_y - d[0]) + min(d[1], size_y // side_y - d[1]),
    )
    fines = []
    pair_counts = jnp.zeros((OWN0, k1), F32)
    for n, (dx, dy) in enumerate(near_first):
        per = size_y // side_y
        i = lax.rem(lax.div(b, per) + dx, side_y) * per + lax.rem(lax.rem(b, per) + dy, per)
        if n > 0:
            id_arrived(i)
        packed = ids[i]
        fine = lax.shift_right_logical(packed, 10)
        mid = lax.bitwise_and(packed, 1023)
        fines.append(fine)
        here = slice(n * PTS, (n + 1) * PTS)
        cat1[:, here] = one_hot_rows(mid, 0, k1)
        pair_counts = pair_counts + dot(one_hot_rows(fine, b * OWN0, OWN0), cat1[:, here], NT)
    pair_counts = pair_counts.astype(BF16)

    def group_counts(first, last):
        for n in range(first, last):
            cat0[:, (n - first) * PTS : (n - first + 1) * PTS] = one_hot_rows(fines[n], 0, OWN0 * size_y)
        part = dot(cat0[:, : (last - first) * PTS], cat1[:, first * PTS : last * PTS], NT)
        if first == 0:
            group[...] = part
        else:
            group[...] += part

    r_u0[b] = s_u0[pl.ds(pl.multiple_of(b * OWN0, OWN0), OWN0), :]
    arrived(1, r_u0.at[pl.ds(0, size_y - 1)])
    u0 = jnp.sum(r_u0[...].astype(F32), axis=0)
    summed0 = dot_split(u0, up_ref[0])
    inverse0 = inverse_rms(summed0)
    normed0 = summed0 * inverse0
    n0 = normed0.astype(BF16)
    s_u1[...] = dot(pair_counts, n0, TN).astype(BF16)
    exchange("q", 4, lambda i: s_u1.at[pl.ds(i * 16, 16)], r_u1.at[q])
    mine32 = pl.ds(pl.multiple_of(b * OWN0, OWN0), OWN0)
    r_t0[b] = s_t0[mine32, :]
    arrived(3, r_t0.at[pl.ds(0, size_y - 1)])
    t0 = jnp.sum(r_t0[...].astype(F32), axis=0)
    ut0[mine32, :C] = u0.astype(BF16)
    ut0[mine32, C:] = t0.astype(BF16)
    exchange("y", 5, lambda i: ut0.at[mine32], ut0.at[mine32])

    mine16 = pl.ds(pl.multiple_of(q * 16, 16), 16)
    r_p1[q] = s_p1[mine16, :]
    arrived(2, r_p1.at[pl.ds(0, size_q - 1)])
    z_p1[z] = jnp.sum(r_p1[...].astype(F32), axis=0).astype(BF16)
    pl.semaphore_wait(relay, 2)
    exchange("z", 6, lambda i: z_p1.at[z], z_p1.at[z])

    for side in range(4):
        got = (
            (fx.at[pl.ds(0, 2)], bx.at[pl.ds(0, 2)])
            if side == 0
            else (fx.at[pl.ds(2, 2)], bx.at[pl.ds(2, 2)])
            if side == 1
            else (fy.at[pl.ds(0, 2)], by.at[pl.ds(0, 2)])
        )

        @pl.when(has[side])
        def _(side=side, got=got):
            for kind in range(2):
                pltpu.make_async_copy(got[kind], got[kind], halo_recv.at[2 * side + kind]).wait()

        @pl.when(jnp.logical_not(has[side]))
        def _(side=side):
            for i in ((0, 1), (2, 3), (0, 2), (1, 3))[side]:
                for ref in ((fx, bx) if side < 2 else (fy, by)):
                    ref[i] = jnp.zeros((BLK, C), BF16)

    for t in range(4):
        total = near[t] + dot(halo_ref[2 * t], fx[t]) + dot(halo_ref[2 * t + 1], fy[t])
        nv[pl.ds(t * BLK, BLK), :] = total.astype(BF16)
        ret[t] = ret[t] + bx[t].astype(F32) + by[t].astype(F32)
    near_part = dot(nv[...], cot, TN)
    down0_part = dot(n0, t0.astype(BF16), TN)
    s_p2[...] = jnp.concatenate(
        [near_part.reshape(size_y, 8, C), down0_part.reshape(size_y, 8, C)], axis=1
    ).astype(BF16)
    exchange("q", 7, lambda i: s_p2.at[lax.rem(i, size_y)], r_p2.at[q])

    third = (size_y + 2) // 3
    group_counts(0, third)

    r_u1[q] = s_u1[mine16, :]
    arrived(4, r_u1.at[pl.ds(0, size_q - 1)])
    z_u1[z] = jnp.sum(r_u1[...].astype(F32), axis=0).astype(BF16)
    exchange("z", 8, lambda i: z_u1.at[z], z_u1.at[z])

    r_p2[q] = s_p2[b]
    arrived(7, r_p2.at[pl.ds(0, size_q - 1)])
    z_p2[z] = jnp.sum(r_p2[...].astype(F32), axis=0).astype(BF16)
    exchange("z", 10, lambda i: z_p2.at[z], z_p2.at[z])
    group_counts(third, 2 * third)

    arrived(6, z_p1.at[pl.ds(0, size_z - 1)])
    p1[mine16, :] = jnp.sum(z_p1[...].astype(F32), axis=0).astype(BF16)
    exchange("q", 9, lambda i: p1.at[mine16], p1.at[mine16])

    group_counts(2 * third, size_y)
    group_bf[...] = group[...].astype(BF16)
    arrived(5, ut0.at[pl.ds(0, (size_y - 1) * OWN0)])
    u0_t[...] = ut0[:, :C].astype(F32).T.astype(BF16)
    summed0 = dot(ut0[:, :C], up_ref[0])
    inverse0 = inverse_rms(summed0)
    normed0 = summed0 * inverse0
    raw0 = dot(ut0[:, C:], dn_ref[0], NT)

    arrived(8, z_u1.at[pl.ds(0, size_z - 1)])
    u1[mine16, :] = jnp.sum(z_u1[...].astype(F32), axis=0).astype(BF16)
    exchange("q", 11, lambda i: u1.at[mine16], u1.at[mine16])

    combined = points.astype(F32) + dot(nv[...], nw_ref[...])
    combined = combined + dot(dot(ot0[...], normed0.astype(BF16), TN).astype(BF16), dn_ref[0])
    arrived(10, z_p2.at[pl.ds(0, size_z - 1)])
    g_p2[b] = jnp.sum(z_p2[...].astype(F32), axis=0) * scale
    exchange("y", 12, lambda i: g_p2.at[b], g_p2.at[b])

    arrived(9, p1.at[pl.ds(0, (size_q - 1) * 16)])
    t1 = p1[:, :C]
    upper_part = p1[:k2, C:].astype(F32)
    t2 = jnp.where(lane < k2, pltpu.roll(upper_part, C - k2, 1), p1[k2 : 2 * k2, C:].astype(F32))
    t2 = t2.astype(BF16)
    counts = p1[:, C:][:, :k2]
    counts_t = counts.astype(F32).T.astype(BF16)

    raw2 = dot(t2, dn_ref[2], NT)
    raw1 = dot(t1, dn_ref[1], NT)
    arrived(11, u1.at[pl.ds(0, (size_q - 1) * 16)])
    summed1 = dot(u1[...], up_ref[1])
    inverse1 = inverse_rms(summed1)
    normed1 = summed1 * inverse1
    n1 = normed1.astype(BF16)
    u2 = dot(counts_t, n1)
    summed2 = dot_split(u2, up_ref[2])
    inverse2 = inverse_rms(summed2)
    normed2 = summed2 * inverse2
    n2 = normed2.astype(BF16)
    sg2 = norm_back(raw2, normed2, inverse2).astype(BF16)
    back2 = dot(sg2, up_ref[2], NT)
    back2_high = back2.astype(BF16)
    back2_low = (back2 - back2_high.astype(F32)).astype(BF16)
    raw1 = raw1 + dot(counts, back2_high) + dot(counts, back2_low)
    sg1 = norm_back(raw1, normed1, inverse1).astype(BF16)
    raw0 = raw0 + dot_split(dot(group_bf[...], sg1), up_ref[1], NT)
    sg0 = norm_back(raw0, normed0, inverse0).astype(BF16)
    s_d[...] = dot(u0_t[...], sg0).reshape(size_y, 8, C)
    to_pair = pltpu.make_async_remote_copy(
        src_ref=s_d.at[b],
        dst_ref=r_d,
        send_sem=send_sem.at[13],
        recv_sem=recv_sem.at[13],
        device_id=(a + 1 - 2 * core, b),
        device_id_type=MESH,
    )
    to_pair.start()

    wg_ref[2] = dot(u1[...], sg1, TN) * scale
    wg_ref[3] = dot_split(u2, sg2, TN) * scale
    to_pair.wait()
    z_d[z] = s_d[b] + r_d[...]
    exchange("z", 15, lambda i: z_d.at[z], z_d.at[z])
    wg_ref[5] = dot(n1, t1, TN) * scale
    wg_ref[6] = dot(n2, t2, TN) * scale

    combined = combined + dot(dot(ot1[...], n1, TN).astype(BF16), dn_ref[1])
    combined = combined + dot(dot(ot2[:k2, :], n2, TN).astype(BF16), dn_ref[2])
    mixed_ref[...] = combined.astype(BF16)
    put_mixed = pltpu.make_async_copy(mixed_ref, mixed_out, out_sem.at[0])
    put_mixed.start()

    upper0 = dot(ot0[...], sg0, TN).astype(BF16)
    grad = cot.astype(F32) + ret[...].reshape(PTS, C) + dot(upper0, up_ref[0], NT)
    pg_ref[...] = grad.astype(BF16)
    put_pg = pltpu.make_async_copy(pg_ref, pg_out, out_sem.at[1])
    put_pg.start()

    arrived(12, g_p2.at[pl.ds(0, size_y - 1)])
    wg_ref[0] = g_p2[:, :8, :].reshape(C, C)
    wg_ref[4] = g_p2[:, 8:, :].reshape(C, C)
    put_first = pltpu.make_async_copy(wg_ref.at[0], wg_out.at[0], out_sem.at[2])
    put_first.start()
    put_rest = pltpu.make_async_copy(wg_ref.at[pl.ds(2, 5)], wg_out.at[pl.ds(2, 5)], out_sem.at[3])
    put_rest.start()

    arrived(15, z_d.at[pl.ds(0, size_z - 1)])
    g_d[b] = jnp.sum(z_d[...], axis=0) * scale
    exchange("y", 16, lambda i: g_d.at[b], g_d.at[b])
    for step, ref in (
        (0, ids.at[pl.ds(0, size_y - 1)]),
        (1, r_u0.at[pl.ds(0, size_y - 1)]),
        (2, r_p1.at[pl.ds(0, size_q - 1)]),
        (3, r_t0.at[pl.ds(0, size_y - 1)]),
        (4, r_u1.at[pl.ds(0, size_q - 1)]),
        (5, ut0.at[pl.ds(0, (size_y - 1) * OWN0)]),
        (6, z_p1.at[pl.ds(0, size_z - 1)]),
        (7, r_p2.at[pl.ds(0, size_q - 1)]),
        (8, z_u1.at[pl.ds(0, size_z - 1)]),
        (9, p1.at[pl.ds(0, (size_q - 1) * 16)]),
        (10, z_p2.at[pl.ds(0, size_z - 1)]),
        (11, u1.at[pl.ds(0, (size_q - 1) * 16)]),
        (12, g_p2.at[pl.ds(0, size_y - 1)]),
        (15, z_d.at[pl.ds(0, size_z - 1)]),
    ):
        sent(step, ref)
    for side in range(4):

        @pl.when(has[side])
        def _(side=side):
            for kind in range(2):
                two = fx.at[pl.ds(0, 2)]
                pltpu.make_async_copy(two, two, halo_send.at[2 * side + kind]).wait()

    for put in (put_mixed, put_pg, put_first, put_rest):
        put.wait()
    arrived(16, g_d.at[pl.ds(0, size_y - 1)])
    sent(16, g_d.at[pl.ds(0, size_y - 1)])
    wg_ref[1] = g_d[...].reshape(C, C)
    put_last = pltpu.make_async_copy(wg_ref.at[1], wg_out.at[1], out_sem.at[4])
    put_last.start()
    put_last.wait()


def store(*refs):
    sources, targets, held, sem = refs[:3], refs[3:6], refs[6:9], refs[9]
    first = [pltpu.make_async_copy(sources[i], held[i], sem.at[i]) for i in range(3)]
    then = [pltpu.make_async_copy(held[i], targets[i], sem.at[3 + i]) for i in range(3)]
    for copy in first:
        copy.start()
    for i in range(3):
        first[i].wait()
        then[i].start()
    for copy in then:
        copy.wait()


def on_device(
    size_x,
    size_y,
    points,
    cotangent,
    local_tiles,
    local_source,
    halo_tiles,
    cluster_fine,
    cluster_mid,
    cluster_coarse,
    near_weight,
    up_weights,
    down_weights,
):
    size_z, size_q, k1 = size_x // 2, 2 * size_y, size_x * size_y
    k0 = OWN0 * size_y
    blocks = pltpu.VMEM((4, BLK, C), BF16)
    hbm = pl.BlockSpec(memory_space=pltpu.HBM)
    scratch = [
        pltpu.VMEM((PTS, C), BF16),
        pltpu.VMEM((PTS, C), BF16),
        pltpu.VMEM((7, C, C), F32),
        pltpu.SemaphoreType.DMA((5,)),
        pltpu.VMEM((4, BLK, C), BF16),
        pltpu.VMEM((PTS, C), BF16),
        pltpu.VMEM((PTS, 3 * BLK), BF16),
        pltpu.SMEM((4, 3), jnp.int32),
        pltpu.VMEM((8, BLK, BLK), BF16),
        pltpu.VMEM((1, PTS), jnp.int32),
        pltpu.VMEM((1, PTS), jnp.int32),
        pltpu.VMEM((1, PTS), jnp.int32),
        pltpu.VMEM((C, C), BF16),
        pltpu.VMEM((3, C, C), BF16),
        pltpu.VMEM((3, C, C), BF16),
        pltpu.SemaphoreType.DMA((11,)),
        pltpu.VMEM((k0, PTS), BF16),
        pltpu.VMEM((k1, PTS), BF16),
        pltpu.VMEM((C, PTS), BF16),
        pltpu.VMEM((4, BLK, C), F32),
        pltpu.VMEM((4, BLK, C), F32),
        pltpu.VMEM((PTS, C), BF16),
        blocks,
        blocks,
        blocks,
        blocks,
        blocks,
        blocks,
        pltpu.VMEM((size_y, 1, PTS), jnp.int32),
        pltpu.VMEM((k0, C), BF16),
        pltpu.VMEM((size_y, OWN0, C), BF16),
        pltpu.VMEM((k0, C), BF16),
        pltpu.VMEM((size_y, OWN0, C), BF16),
        pltpu.VMEM((k1, 2 * C), BF16),
        pltpu.VMEM((size_q, 16, 2 * C), BF16),
        pltpu.VMEM((size_z, 16, 2 * C), BF16),
        pltpu.VMEM((k1, 2 * C), BF16),
        pltpu.VMEM((k1, C), BF16),
        pltpu.VMEM((size_q, 16, C), BF16),
        pltpu.VMEM((size_z, 16, C), BF16),
        pltpu.VMEM((k1, C), BF16),
        pltpu.VMEM((k0, 2 * C), BF16),
        pltpu.VMEM((C, k0), BF16),
        pltpu.VMEM((k0, (size_y + 2) // 3 * PTS), BF16),
        pltpu.VMEM((k1, size_y * PTS), BF16),
        pltpu.VMEM((k0, k1), F32),
        pltpu.VMEM((k0, k1), BF16),
        pltpu.VMEM((size_y, 16, C), BF16),
        pltpu.VMEM((size_q, 16, C), BF16),
        pltpu.VMEM((size_z, 16, C), BF16),
        pltpu.VMEM((size_y, 16, C), F32),
        pltpu.VMEM((size_y, 8, C), F32),
        pltpu.VMEM((8, C), F32),
        pltpu.VMEM((size_z, 8, C), F32),
        pltpu.VMEM((size_y, 8, C), F32),
        pltpu.SemaphoreType.DMA((17,)),
        pltpu.SemaphoreType.DMA((17,)),
        pltpu.SemaphoreType.DMA((8,)),
        pltpu.SemaphoreType.DMA((8,)),
        pltpu.SemaphoreType.DMA((size_y,)),
        pltpu.SemaphoreType.REGULAR,
    ]
    outs = pl.pallas_call(
        functools.partial(kernel, size_x, size_y),
        out_shape=(
            jax.ShapeDtypeStruct((PTS, C), BF16),
            jax.ShapeDtypeStruct((PTS, C), BF16),
            jax.ShapeDtypeStruct((7, C, C), F32),
        ),
        in_specs=[hbm] * 11,
        out_specs=(hbm,) * 3,
        scratch_shapes=scratch,
        name="layer",
        compiler_params=pltpu.CompilerParams(
            collective_id=0, has_side_effects=True, vmem_limit_bytes=60 * 1024 * 1024
        ),
    )(
        points.reshape(4, BLK, C),
        cotangent,
        local_tiles,
        local_source,
        halo_tiles.reshape(8, BLK, BLK),
        cluster_fine.reshape(1, PTS),
        cluster_mid.reshape(1, PTS),
        cluster_coarse.reshape(1, PTS),
        near_weight,
        up_weights,
        down_weights,
    )
    return pl.pallas_call(
        store,
        out_shape=tuple(jax.ShapeDtypeStruct(o.shape, o.dtype) for o in outs),
        in_specs=[hbm] * 3,
        out_specs=(hbm,) * 3,
        scratch_shapes=[pltpu.VMEM(o.shape, o.dtype) for o in outs] + [pltpu.SemaphoreType.DMA((6,))],
        name="store",
        compiler_params=pltpu.CompilerParams(vmem_limit_bytes=60 * 1024 * 1024),
    )(*outs)


def solution(mesh):
    rows = P(("gx", "gy"), None)
    flat = P(("gx", "gy"))
    size_x, size_y = mesh.shape["gx"], mesh.shape["gy"]
    return jax.shard_map(
        functools.partial(on_device, size_x, size_y),
        mesh=mesh,
        in_specs=(rows, rows, rows, rows, rows, flat, flat, flat, P(), P(), P()),
        out_specs=(rows, rows, P()),
        check_vma=False,
    )
```

```python
import functools
import math

import jax
import jax.numpy as jnp
from jax import lax
from jax.experimental import pallas as pl
from jax.experimental.pallas import tpu as pltpu
from jax.sharding import PartitionSpec as P

BLK = 128
C = 128
PTS = 512
OWN0 = 32
EPSILON = 1e-05
MESH = pl.DeviceIdType.MESH
F32, BF16 = jnp.float32, jnp.bfloat16

NN = ((1,), (0,))
NT = ((1,), (1,))
TN = ((0,), (0,))


def dot(a, b, dims=NN):
    return lax.dot_general(a, b, (dims, ((), ())), preferred_element_type=F32)


def dot_split(a, b, dims=NN):
    high = a.astype(BF16)
    low = (a - high.astype(F32)).astype(BF16)
    return dot(high, b, dims) + dot(low, b, dims)


def one_hot_rows(ids, first, count):
    rows = lax.broadcasted_iota(jnp.int32, (count, ids.shape[1]), 0) + first
    return jnp.where(rows == ids, 1.0, 0.0).astype(BF16)


def inverse_rms(summed):
    return lax.rsqrt(jnp.mean(summed * summed, axis=-1, keepdims=True) + EPSILON)


def norm_back(raw, normed, inverse):
    return inverse * (raw - normed * jnp.mean(raw * normed, axis=-1, keepdims=True))


def kernel(
    size_x,
    size_y,
    pts_in,
    cot_in,
    tiles_in,
    src_in,
    halo_in,
    c0_in,
    c1_in,
    c2_in,
    nw_in,
    up_in,
    dn_in,
    mixed_out,
    pg_out,
    wg_out,
    mixed_ref,
    pg_ref,
    wg_ref,
    out_sem,
    pts_ref,
    cot_ref,
    tiles_ref,
    src_ref,
    halo_ref,
    c0_ref,
    c1_ref,
    c2_ref,
    nw_ref,
    up_ref,
    dn_ref,
    load_sem,
    ot0,
    ot1,
    ot2,
    near,
    ret,
    nv,
    spx,
    spy,
    fx,
    fy,
    bx,
    by,
    ids,
    s_u0,
    r_u0,
    s_t0,
    r_t0,
    s_p1,
    r_p1,
    n_p1,
    f_p1,
    p1,
    s_u1,
    r_u1,
    z_u1,
    u1,
    ut0,
    u0_t,
    cat0,
    cat1,
    group,
    group_bf,
    s_p2,
    r_p2,
    z_p2,
    g_p2,
    s_d,
    r_d,
    z_d,
    send_sem,
    recv_sem,
    halo_send,
    halo_recv,
    ids_recv,
    relay,
):
    size_z = size_x // 2
    size_q = 2 * size_y
    k1 = size_x * size_y
    k2 = k1 // 8
    a = lax.axis_index("gx")
    b = lax.axis_index("gy")
    z = lax.div(a, 2)
    core = lax.rem(a, 2)
    q = core * size_y + b
    scale = 1.0 / math.sqrt(PTS * size_x * size_y)

    def peer(kind, o):
        if kind == "y":
            i = lax.rem(b + o, size_y)
            return i, (a, i)
        if kind == "z":
            i = lax.rem(z + o, size_z)
            return i, (i * 2 + core, b)
        if kind == "near":
            i = lax.rem(z + o, 4)
            return i, ((z - lax.rem(z, 4) + i) * 2 + core, b)
        if kind == "far":
            i = lax.rem(z + 4 * o, size_z)
            return lax.div(i, 4), (i * 2 + core, b)
        i = lax.rem(q + o, size_q)
        return i, (z * 2 + lax.div(i, size_y), lax.rem(i, size_y))

    count = {"y": size_y, "z": size_z, "q": size_q, "near": 4, "far": size_z // 4}

    def exchange(kind, step, source, target, landed=None):
        def body(o, carry):
            i, device = peer(kind, o)
            pltpu.make_async_remote_copy(
                src_ref=source(i),
                dst_ref=target,
                send_sem=send_sem.at[step],
                recv_sem=recv_sem.at[step] if landed is None else landed,
                device_id=device,
                device_id_type=MESH,
            ).start()
            return carry

        lax.fori_loop(1, count[kind], body, 0)

    def arrived(step, ref):
        pltpu.make_async_copy(ref, ref, recv_sem.at[step]).wait()

    def id_arrived(i):
        pltpu.make_async_copy(ids.at[i], ids.at[i], ids_recv.at[i]).wait()

    def sent(step, ref):
        pltpu.make_async_copy(ref, ref, send_sem.at[step]).wait()

    loads = {
        name: pltpu.make_async_copy(source, target, load_sem.at[i])
        for i, (name, source, target) in enumerate(
            (
                ("c0", c0_in, c0_ref),
                ("pts", pts_in, pts_ref),
                ("cot", cot_in, cot_ref),
                ("c1", c1_in, c1_ref),
                ("c2", c2_in, c2_ref),
                ("nw", nw_in, nw_ref),
                ("src", src_in, src_ref),
                ("tiles", tiles_in, tiles_ref),
                ("halo", halo_in, halo_ref),
                ("up", up_in, up_ref),
                ("dn", dn_in, dn_ref),
            )
        )
    }
    barrier = pltpu.get_barrier_semaphore()

    reach = size_z // 4

    def greet(kind, steps, shift):
        def body(o, carry):
            _, device = peer(kind, o + shift)
            pl.semaphore_signal(barrier, inc=1, device_id=device, device_id_type=MESH)
            return carry

        lax.fori_loop(1, steps + 1, body, 0)

    greet("z", reach, 0)
    greet("z", reach, size_z - reach - 1)
    greet("q", size_q - 1, 0)
    beside = lax.rem(a + size_x - 1 + 2 * core, size_x)
    pl.semaphore_signal(barrier, inc=1, device_id=(beside, b), device_id_type=MESH)

    for load in loads.values():
        load.start()

    for name in ("c0", "pts", "cot", "c1", "c2"):
        loads[name].wait()
    points = pts_ref[...].reshape(PTS, C)
    cot = cot_ref[...]
    c0, c1, c2 = c0_ref[...], c1_ref[...], c2_ref[...]
    ot0[...] = one_hot_rows(c0, 0, OWN0 * size_y)
    ot1[...] = one_hot_rows(c1, 0, k1)
    ot2[...] = one_hot_rows(c2, 0, C)
    both = dot(ot0[...], jnp.concatenate([points, cot], axis=1))
    s_u0[...] = both[:, :C].astype(BF16)
    s_t0[...] = both[:, C:].astype(BF16)
    ids[b] = c0 * 1024 + c1
    lane = lax.broadcasted_iota(jnp.int32, (k2, C), 1)
    t2 = dot(ot2[...], cot)[:k2]
    s_p1[:, :C] = dot(ot1[...], cot).astype(BF16)
    counts = dot(ot1[...], ot2[...], NT)
    s_p1[2 * k2 :, C:] = counts[2 * k2 :].astype(BF16)
    s_p1[:k2, C:] = jnp.where(lane < k2, counts[:k2], pltpu.roll(t2, C - k2, 1)).astype(BF16)
    s_p1[k2 : 2 * k2, C:] = jnp.where(lane < k2, counts[k2 : 2 * k2], t2).astype(BF16)

    for name in ("nw", "src", "tiles", "halo", "up", "dn"):
        loads[name].wait()
    near_grad = dot(cot, nw_ref[...], NT).astype(BF16)
    returned = [jnp.zeros((BLK, C), F32)] * 4
    for t in range(4):
        rows = slice(t * BLK, (t + 1) * BLK)
        tile = tiles_ref[rows, :]
        sources = jnp.concatenate([pts_ref[src_ref[t, k]] for k in range(3)], axis=0)
        near[t] = dot(tile, sources)
        grad = near_grad[rows]
        pieces = dot(tile, grad, TN)
        for k in range(3):
            piece = pieces[k * BLK : (k + 1) * BLK]
            for s in range(4):
                returned[s] = returned[s] + jnp.where(src_ref[t, k] == s, piece, 0.0)
        spx[t] = dot(halo_ref[2 * t], grad, TN).astype(BF16)
        spy[t] = dot(halo_ref[2 * t + 1], grad, TN).astype(BF16)
    for s in range(4):
        ret[s] = returned[s]

    pl.semaphore_wait(barrier, 2 * reach + size_q - 1 + 1)
    for o in (reach, size_z - reach):
        _, device = peer("z", o)
        pl.semaphore_signal(relay, inc=1, device_id=device, device_id_type=MESH)

    exchange("y", 0, lambda i: ids.at[b], ids.at[b], ids_recv.at[b])
    exchange("y", 1, lambda i: s_u0.at[pl.ds(i * OWN0, OWN0)], r_u0.at[b])
    exchange("q", 2, lambda i: s_p1.at[pl.ds(i * 16, 16)], r_p1.at[q])
    has = (a > 0, a < size_x - 1, b > 0, b < size_y - 1)

    def halo_copies(side):
        if side == 0:
            return [[(pts_ref.at[pl.ds(0, 2)], fx.at[pl.ds(2, 2)])], [(spx.at[pl.ds(0, 2)], bx.at[pl.ds(2, 2)])]]
        if side == 1:
            return [[(pts_ref.at[pl.ds(2, 2)], fx.at[pl.ds(0, 2)])], [(spx.at[pl.ds(2, 2)], bx.at[pl.ds(0, 2)])]]
        if side == 2:
            return [[(pts_ref.at[i], fy.at[i + 1]) for i in (0, 2)], [(spy.at[i], by.at[i + 1]) for i in (0, 2)]]
        return [[(pts_ref.at[i], fy.at[i - 1]) for i in (1, 3)], [(spy.at[i], by.at[i - 1]) for i in (1, 3)]]

    neighbour = ((a - 1, b), (a + 1, b), (a, b - 1), (a, b + 1))
    landing = ((fx, bx, 0, 2), (fx, bx, 2, 4), (fy, by, 0, 2), (fy, by, 2, 4))
    edge = ((0, 1), (2, 3), (0, 2), (1, 3))

    def send_halo(kind):
        for side in range(4):

            @pl.when(has[side])
            def _(side=side):
                for source, target in halo_copies(side)[kind]:
                    pltpu.make_async_remote_copy(
                        src_ref=source,
                        dst_ref=target,
                        send_sem=halo_send.at[2 * side + kind],
                        recv_sem=halo_recv.at[2 * (side ^ 1) + kind],
                        device_id=neighbour[side],
                        device_id_type=MESH,
                    ).start()

    def wait_halo(kind):
        for side in range(4):
            ref = landing[side][kind]

            @pl.when(has[side])
            def _(side=side, ref=ref):
                two = ref.at[pl.ds(landing[side][2], 2)]
                pltpu.make_async_copy(two, two, halo_recv.at[2 * side + kind]).wait()

            @pl.when(jnp.logical_not(has[side]))
            def _(side=side, ref=ref):
                for i in edge[side]:
                    ref[i] = jnp.zeros((BLK, C), BF16)

    side_y = math.isqrt(size_y)
    near_first = sorted(
        ((dx, dy) for dx in range(side_y) for dy in range(size_y // side_y)),
        key=lambda d: min(d[0], side_y - d[0]) + min(d[1], size_y // side_y - d[1]),
    )
    fines = []
    pair_counts = jnp.zeros((OWN0, k1), F32)
    for n, (dx, dy) in enumerate(near_first):
        per = size_y // side_y
        i = lax.rem(lax.div(b, per) + dx, side_y) * per + lax.rem(lax.rem(b, per) + dy, per)
        if n > 0:
            id_arrived(i)
        packed = ids[i]
        fine = lax.shift_right_logical(packed, 10)
        mid = lax.bitwise_and(packed, 1023)
        fines.append(fine)
        here = slice(n * PTS, (n + 1) * PTS)
        cat1[:, here] = one_hot_rows(mid, 0, k1)
        pair_counts = pair_counts + dot(one_hot_rows(fine, b * OWN0, OWN0), cat1[:, here], NT)
    pair_counts = pair_counts.astype(BF16)

    def group_counts(first, last):
        for n in range(first, last):
            cat0[:, (n - first) * PTS : (n - first + 1) * PTS] = one_hot_rows(fines[n], 0, OWN0 * size_y)
        part = dot(cat0[:, : (last - first) * PTS], cat1[:, first * PTS : last * PTS], NT)
        if first == 0:
            group[...] = part
        else:
            group[...] += part

    r_u0[b] = s_u0[pl.ds(pl.multiple_of(b * OWN0, OWN0), OWN0), :]
    arrived(1, r_u0.at[pl.ds(0, size_y - 1)])
    u0 = jnp.sum(r_u0[...].astype(F32), axis=0)
    summed0 = dot_split(u0, up_ref[0])
    inverse0 = inverse_rms(summed0)
    normed0 = summed0 * inverse0
    n0 = normed0.astype(BF16)
    s_u1[...] = dot(pair_counts, n0, TN).astype(BF16)
    exchange("q", 4, lambda i: s_u1.at[pl.ds(i * 16, 16)], r_u1.at[q])
    mine32 = pl.ds(pl.multiple_of(b * OWN0, OWN0), OWN0)
    exchange("y", 3, lambda i: s_t0.at[pl.ds(i * OWN0, OWN0)], r_t0.at[b])

    mine16 = pl.ds(pl.multiple_of(q * 16, 16), 16)
    r_p1[q] = s_p1[mine16, :]
    arrived(2, r_p1.at[pl.ds(0, size_q - 1)])
    z_near, z_far = lax.rem(z, 4), lax.div(z, 4)
    n_p1[z_near] = jnp.sum(r_p1[...].astype(F32), axis=0).astype(BF16)
    pl.semaphore_wait(relay, 2)
    exchange("near", 6, lambda i: n_p1.at[z_near], n_p1.at[z_near])

    third = (size_y + 2) // 3
    group_counts(0, third)

    arrived(6, n_p1.at[pl.ds(0, 3)])
    f_p1[z_far] = jnp.sum(n_p1[...].astype(F32), axis=0).astype(BF16)
    exchange("far", 14, lambda i: f_p1.at[z_far], f_p1.at[z_far])

    r_u1[q] = s_u1[mine16, :]
    arrived(4, r_u1.at[pl.ds(0, size_q - 1)])
    z_u1[z] = jnp.sum(r_u1[...].astype(F32), axis=0).astype(BF16)
    exchange("z", 8, lambda i: z_u1.at[z], z_u1.at[z])

    r_t0[b] = s_t0[mine32, :]
    arrived(3, r_t0.at[pl.ds(0, size_y - 1)])
    t0 = jnp.sum(r_t0[...].astype(F32), axis=0)
    ut0[mine32, :C] = u0.astype(BF16)
    ut0[mine32, C:] = t0.astype(BF16)
    exchange("y", 5, lambda i: ut0.at[mine32], ut0.at[mine32])
    send_halo(0)
    group_counts(third, 2 * third)

    wait_halo(0)
    for t in range(4):
        total = near[t] + dot(halo_ref[2 * t], fx[t]) + dot(halo_ref[2 * t + 1], fy[t])
        nv[pl.ds(t * BLK, BLK), :] = total.astype(BF16)
    near_part = dot(nv[...], cot, TN)
    down0_part = dot(n0, t0.astype(BF16), TN)
    s_p2[...] = jnp.concatenate(
        [near_part.reshape(size_y, 8, C), down0_part.reshape(size_y, 8, C)], axis=1
    ).astype(BF16)
    exchange("q", 7, lambda i: s_p2.at[lax.rem(i, size_y)], r_p2.at[q])

    arrived(5, ut0.at[pl.ds(0, (size_y - 1) * OWN0)])
    u0_t[...] = ut0[:, :C].astype(F32).T.astype(BF16)
    summed0 = dot(ut0[:, :C], up_ref[0])
    inverse0 = inverse_rms(summed0)
    normed0 = summed0 * inverse0
    raw0 = dot(ut0[:, C:], dn_ref[0], NT)

    arrived(14, f_p1.at[pl.ds(0, size_z // 4 - 1)])
    p1[mine16, :] = jnp.sum(f_p1[...].astype(F32), axis=0).astype(BF16)
    exchange("q", 9, lambda i: p1.at[mine16], p1.at[mine16])

    arrived(8, z_u1.at[pl.ds(0, size_z - 1)])
    u1[mine16, :] = jnp.sum(z_u1[...].astype(F32), axis=0).astype(BF16)
    exchange("q", 11, lambda i: u1.at[mine16], u1.at[mine16])

    group_counts(2 * third, size_y)
    group_bf[...] = group[...].astype(BF16)
    combined = points.astype(F32) + dot(nv[...], nw_ref[...])
    combined = combined + dot(dot(ot0[...], normed0.astype(BF16), TN).astype(BF16), dn_ref[0])
    arrived(9, p1.at[pl.ds(0, (size_q - 1) * 16)])
    t1 = p1[:, :C]
    upper_part = p1[:k2, C:].astype(F32)
    t2 = jnp.where(lane < k2, pltpu.roll(upper_part, C - k2, 1), p1[k2 : 2 * k2, C:].astype(F32))
    t2 = t2.astype(BF16)
    counts = p1[:, C:][:, :k2]
    counts_t = counts.astype(F32).T.astype(BF16)

    r_p2[q] = s_p2[b]
    arrived(7, r_p2.at[pl.ds(0, size_q - 1)])
    z_p2[z] = jnp.sum(r_p2[...].astype(F32), axis=0).astype(BF16)
    exchange("z", 10, lambda i: z_p2.at[z], z_p2.at[z])

    raw2 = dot(t2, dn_ref[2], NT)
    raw1 = dot(t1, dn_ref[1], NT)
    arrived(11, u1.at[pl.ds(0, (size_q - 1) * 16)])
    summed1 = dot(u1[...], up_ref[1])
    inverse1 = inverse_rms(summed1)
    normed1 = summed1 * inverse1
    n1 = normed1.astype(BF16)
    u2 = dot(counts_t, n1)
    summed2 = dot_split(u2, up_ref[2])
    inverse2 = inverse_rms(summed2)
    normed2 = summed2 * inverse2
    n2 = normed2.astype(BF16)
    sg2 = norm_back(raw2, normed2, inverse2).astype(BF16)
    back2 = dot(sg2, up_ref[2], NT)
    back2_high = back2.astype(BF16)
    back2_low = (back2 - back2_high.astype(F32)).astype(BF16)
    raw1 = raw1 + dot(counts, back2_high) + dot(counts, back2_low)
    sg1 = norm_back(raw1, normed1, inverse1).astype(BF16)
    raw0 = raw0 + dot_split(dot(group_bf[...], sg1), up_ref[1], NT)
    sg0 = norm_back(raw0, normed0, inverse0).astype(BF16)
    s_d[...] = dot(u0_t[...], sg0).reshape(size_y, 8, C)
    to_pair = pltpu.make_async_remote_copy(
        src_ref=s_d.at[b],
        dst_ref=r_d,
        send_sem=send_sem.at[13],
        recv_sem=recv_sem.at[13],
        device_id=(a + 1 - 2 * core, b),
        device_id_type=MESH,
    )
    to_pair.start()

    wg_ref[2] = dot(u1[...], sg1, TN) * scale
    wg_ref[3] = dot_split(u2, sg2, TN) * scale
    to_pair.wait()
    z_d[z] = s_d[b] + r_d[...]
    exchange("z", 15, lambda i: z_d.at[z], z_d.at[z])
    send_halo(1)
    wg_ref[5] = dot(n1, t1, TN) * scale
    wg_ref[6] = dot(n2, t2, TN) * scale

    arrived(10, z_p2.at[pl.ds(0, size_z - 1)])
    g_p2[b] = jnp.sum(z_p2[...].astype(F32), axis=0) * scale
    exchange("y", 12, lambda i: g_p2.at[b], g_p2.at[b])

    combined = combined + dot(dot(ot1[...], n1, TN).astype(BF16), dn_ref[1])
    combined = combined + dot(dot(ot2[:k2, :], n2, TN).astype(BF16), dn_ref[2])
    mixed_ref[...] = combined.astype(BF16)
    put_mixed = pltpu.make_async_copy(mixed_ref, mixed_out, out_sem.at[0])
    put_mixed.start()

    wait_halo(1)
    for t in range(4):
        ret[t] = ret[t] + bx[t].astype(F32) + by[t].astype(F32)
    upper0 = dot(ot0[...], sg0, TN).astype(BF16)
    grad = cot.astype(F32) + ret[...].reshape(PTS, C) + dot(upper0, up_ref[0], NT)
    pg_ref[...] = grad.astype(BF16)
    put_pg = pltpu.make_async_copy(pg_ref, pg_out, out_sem.at[1])
    put_pg.start()

    arrived(12, g_p2.at[pl.ds(0, size_y - 1)])
    wg_ref[0] = g_p2[:, :8, :].reshape(C, C)
    wg_ref[4] = g_p2[:, 8:, :].reshape(C, C)
    put_first = pltpu.make_async_copy(wg_ref.at[0], wg_out.at[0], out_sem.at[2])
    put_first.start()
    put_rest = pltpu.make_async_copy(wg_ref.at[pl.ds(2, 5)], wg_out.at[pl.ds(2, 5)], out_sem.at[3])
    put_rest.start()

    arrived(15, z_d.at[pl.ds(0, size_z - 1)])
    mine8 = pl.ds(pl.multiple_of(b * 8, 8), 8)
    wg_ref[1, mine8, :] = jnp.sum(z_d[...], axis=0) * scale
    exchange("y", 16, lambda i: wg_ref.at[1, mine8], wg_ref.at[1, mine8])
    for step, ref in (
        (0, ids.at[pl.ds(0, size_y - 1)]),
        (1, r_u0.at[pl.ds(0, size_y - 1)]),
        (2, r_p1.at[pl.ds(0, size_q - 1)]),
        (3, r_t0.at[pl.ds(0, size_y - 1)]),
        (4, r_u1.at[pl.ds(0, size_q - 1)]),
        (5, ut0.at[pl.ds(0, (size_y - 1) * OWN0)]),
        (6, n_p1.at[pl.ds(0, 3)]),
        (14, f_p1.at[pl.ds(0, size_z // 4 - 1)]),
        (7, r_p2.at[pl.ds(0, size_q - 1)]),
        (8, z_u1.at[pl.ds(0, size_z - 1)]),
        (9, p1.at[pl.ds(0, (size_q - 1) * 16)]),
        (10, z_p2.at[pl.ds(0, size_z - 1)]),
        (11, u1.at[pl.ds(0, (size_q - 1) * 16)]),
        (12, g_p2.at[pl.ds(0, size_y - 1)]),
        (15, z_d.at[pl.ds(0, size_z - 1)]),
    ):
        sent(step, ref)
    for side in range(4):

        @pl.when(has[side])
        def _(side=side):
            for kind in range(2):
                two = fx.at[pl.ds(0, 2)]
                pltpu.make_async_copy(two, two, halo_send.at[2 * side + kind]).wait()

    for put in (put_mixed, put_pg, put_first, put_rest):
        put.wait()
    arrived(16, wg_ref.at[1, pl.ds(0, (size_y - 1) * 8)])
    sent(16, wg_ref.at[1, pl.ds(0, (size_y - 1) * 8)])
    put_last = pltpu.make_async_copy(wg_ref.at[1], wg_out.at[1], out_sem.at[4])
    put_last.start()
    put_last.wait()


def store(*refs):
    sources, targets, held, sem = refs[:3], refs[3:6], refs[6:9], refs[9]
    first = [pltpu.make_async_copy(sources[i], held[i], sem.at[i]) for i in range(3)]
    then = [pltpu.make_async_copy(held[i], targets[i], sem.at[3 + i]) for i in range(3)]
    for copy in first:
        copy.start()
    for i in range(3):
        first[i].wait()
        then[i].start()
    for copy in then:
        copy.wait()


def on_device(
    size_x,
    size_y,
    points,
    cotangent,
    local_tiles,
    local_source,
    halo_tiles,
    cluster_fine,
    cluster_mid,
    cluster_coarse,
    near_weight,
    up_weights,
    down_weights,
):
    size_z, size_q, k1 = size_x // 2, 2 * size_y, size_x * size_y
    k0 = OWN0 * size_y
    blocks = pltpu.VMEM((4, BLK, C), BF16)
    hbm = pl.BlockSpec(memory_space=pltpu.HBM)
    scratch = [
        pltpu.VMEM((PTS, C), BF16),
        pltpu.VMEM((PTS, C), BF16),
        pltpu.VMEM((7, C, C), F32),
        pltpu.SemaphoreType.DMA((5,)),
        pltpu.VMEM((4, BLK, C), BF16),
        pltpu.VMEM((PTS, C), BF16),
        pltpu.VMEM((PTS, 3 * BLK), BF16),
        pltpu.SMEM((4, 3), jnp.int32),
        pltpu.VMEM((8, BLK, BLK), BF16),
        pltpu.VMEM((1, PTS), jnp.int32),
        pltpu.VMEM((1, PTS), jnp.int32),
        pltpu.VMEM((1, PTS), jnp.int32),
        pltpu.VMEM((C, C), BF16),
        pltpu.VMEM((3, C, C), BF16),
        pltpu.VMEM((3, C, C), BF16),
        pltpu.SemaphoreType.DMA((11,)),
        pltpu.VMEM((k0, PTS), BF16),
        pltpu.VMEM((k1, PTS), BF16),
        pltpu.VMEM((C, PTS), BF16),
        pltpu.VMEM((4, BLK, C), F32),
        pltpu.VMEM((4, BLK, C), F32),
        pltpu.VMEM((PTS, C), BF16),
        blocks,
        blocks,
        blocks,
        blocks,
        blocks,
        blocks,
        pltpu.VMEM((size_y, 1, PTS), jnp.int32),
        pltpu.VMEM((k0, C), BF16),
        pltpu.VMEM((size_y, OWN0, C), BF16),
        pltpu.VMEM((k0, C), BF16),
        pltpu.VMEM((size_y, OWN0, C), BF16),
        pltpu.VMEM((k1, 2 * C), BF16),
        pltpu.VMEM((size_q, 16, 2 * C), BF16),
        pltpu.VMEM((4, 16, 2 * C), BF16),
        pltpu.VMEM((size_z // 4, 16, 2 * C), BF16),
        pltpu.VMEM((k1, 2 * C), BF16),
        pltpu.VMEM((k1, C), BF16),
        pltpu.VMEM((size_q, 16, C), BF16),
        pltpu.VMEM((size_z, 16, C), BF16),
        pltpu.VMEM((k1, C), BF16),
        pltpu.VMEM((k0, 2 * C), BF16),
        pltpu.VMEM((C, k0), BF16),
        pltpu.VMEM((k0, (size_y + 2) // 3 * PTS), BF16),
        pltpu.VMEM((k1, size_y * PTS), BF16),
        pltpu.VMEM((k0, k1), F32),
        pltpu.VMEM((k0, k1), BF16),
        pltpu.VMEM((size_y, 16, C), BF16),
        pltpu.VMEM((size_q, 16, C), BF16),
        pltpu.VMEM((size_z, 16, C), BF16),
        pltpu.VMEM((size_y, 16, C), F32),
        pltpu.VMEM((size_y, 8, C), F32),
        pltpu.VMEM((8, C), F32),
        pltpu.VMEM((size_z, 8, C), F32),
        pltpu.SemaphoreType.DMA((17,)),
        pltpu.SemaphoreType.DMA((17,)),
        pltpu.SemaphoreType.DMA((8,)),
        pltpu.SemaphoreType.DMA((8,)),
        pltpu.SemaphoreType.DMA((size_y,)),
        pltpu.SemaphoreType.REGULAR,
    ]
    outs = pl.pallas_call(
        functools.partial(kernel, size_x, size_y),
        out_shape=(
            jax.ShapeDtypeStruct((PTS, C), BF16),
            jax.ShapeDtypeStruct((PTS, C), BF16),
            jax.ShapeDtypeStruct((7, C, C), F32),
        ),
        in_specs=[hbm] * 11,
        out_specs=(hbm,) * 3,
        scratch_shapes=scratch,
        name="layer",
        compiler_params=pltpu.CompilerParams(
            collective_id=0, has_side_effects=True, vmem_limit_bytes=60 * 1024 * 1024
        ),
    )(
        points.reshape(4, BLK, C),
        cotangent,
        local_tiles,
        local_source,
        halo_tiles.reshape(8, BLK, BLK),
        cluster_fine.reshape(1, PTS),
        cluster_mid.reshape(1, PTS),
        cluster_coarse.reshape(1, PTS),
        near_weight,
        up_weights,
        down_weights,
    )
    return pl.pallas_call(
        store,
        out_shape=tuple(jax.ShapeDtypeStruct(o.shape, o.dtype) for o in outs),
        in_specs=[hbm] * 3,
        out_specs=(hbm,) * 3,
        scratch_shapes=[pltpu.VMEM(o.shape, o.dtype) for o in outs] + [pltpu.SemaphoreType.DMA((6,))],
        name="store",
        compiler_params=pltpu.CompilerParams(vmem_limit_bytes=60 * 1024 * 1024),
    )(*outs)


def solution(mesh):
    rows = P(("gx", "gy"), None)
    flat = P(("gx", "gy"))
    size_x, size_y = mesh.shape["gx"], mesh.shape["gy"]
    return jax.shard_map(
        functools.partial(on_device, size_x, size_y),
        mesh=mesh,
        in_specs=(rows, rows, rows, rows, rows, flat, flat, flat, P(), P(), P()),
        out_specs=(rows, rows, P()),
        check_vma=False,
    )
```

```python
import functools
import math

import jax
import jax.numpy as jnp
from jax import lax
from jax.experimental import pallas as pl
from jax.experimental.pallas import tpu as pltpu
from jax.sharding import PartitionSpec as P

BLK = 128
C = 128
PTS = 512
OWN0 = 32
EPSILON = 1e-05
MESH = pl.DeviceIdType.MESH
F32, BF16 = jnp.float32, jnp.bfloat16

NN = ((1,), (0,))
NT = ((1,), (1,))
TN = ((0,), (0,))


def dot(a, b, dims=NN):
    return lax.dot_general(a, b, (dims, ((), ())), preferred_element_type=F32)


def dot_split(a, b, dims=NN):
    high = a.astype(BF16)
    low = (a - high.astype(F32)).astype(BF16)
    return dot(high, b, dims) + dot(low, b, dims)


def one_hot_rows(ids, first, count):
    rows = lax.broadcasted_iota(jnp.int32, (count, ids.shape[1]), 0) + first
    return jnp.where(rows == ids, 1.0, 0.0).astype(BF16)


def inverse_rms(summed):
    return lax.rsqrt(jnp.mean(summed * summed, axis=-1, keepdims=True) + EPSILON)


def norm_back(raw, normed, inverse):
    return inverse * (raw - normed * jnp.mean(raw * normed, axis=-1, keepdims=True))


def kernel(
    size_x,
    size_y,
    pts_in,
    cot_in,
    tiles_in,
    src_in,
    halo_in,
    c0_in,
    c1_in,
    c2_in,
    nw_in,
    up_in,
    dn_in,
    mixed_out,
    pg_out,
    wg_out,
    mixed_ref,
    pg_ref,
    wg_ref,
    out_sem,
    pts_ref,
    cot_ref,
    tiles_ref,
    src_ref,
    halo_ref,
    c0_ref,
    c1_ref,
    c2_ref,
    nw_ref,
    up_ref,
    dn_ref,
    load_sem,
    ot0,
    ot1,
    ot2,
    near,
    ret,
    nv,
    spx,
    spy,
    fx,
    fy,
    bx,
    by,
    ids,
    s_u0,
    r_u0,
    s_t0,
    r_t0,
    s_p1,
    r_p1,
    n_p1,
    f_p1,
    p1,
    s_u1,
    r_u1,
    z_u1,
    u1,
    ut0,
    u0_t,
    cat0,
    cat1,
    group,
    group_bf,
    s_p2,
    r_p2,
    z_p2,
    g_p2,
    s_d,
    r_d,
    z_d,
    send_sem,
    recv_sem,
    halo_send,
    halo_recv,
    ids_recv,
    relay,
):
    size_z = size_x // 2
    size_q = 2 * size_y
    k1 = size_x * size_y
    k2 = k1 // 8
    a = lax.axis_index("gx")
    b = lax.axis_index("gy")
    z = lax.div(a, 2)
    core = lax.rem(a, 2)
    q = core * size_y + b
    scale = 1.0 / math.sqrt(PTS * size_x * size_y)

    side_y = math.isqrt(size_y)
    side_x = size_y // side_y

    def in_plane(o):
        x = lax.rem(lax.div(b, side_x) + lax.div(o, side_x), side_y)
        return x * side_x + lax.rem(lax.rem(b, side_x) + lax.rem(o, side_x), side_x)

    def peer(kind, o):
        if kind == "y":
            i = in_plane(o)
            return i, (a, i)
        if kind == "z":
            i = lax.rem(z + o, size_z)
            return i, (i * 2 + core, b)
        if kind == "near":
            i = lax.rem(z + o, 4)
            return i, ((z - lax.rem(z, 4) + i) * 2 + core, b)
        if kind == "far":
            i = lax.rem(z + 4 * o, size_z)
            return lax.div(i, 4), (i * 2 + core, b)
        c = lax.rem(core + o, 2)
        i = in_plane(lax.div(o, 2))
        return c * size_y + i, (z * 2 + c, i)

    farthest = {
        "y": size_y // 2 + side_x // 2,
        "z": size_z // 2,
        "q": size_y + 2 * (side_x // 2),
        "near": 2,
        "far": size_z // 8,
    }
    count = {"y": size_y, "z": size_z, "q": size_q, "near": 4, "far": size_z // 4}

    def exchange(kind, step, source, target, landed=None):
        late = count[kind] - farthest[kind]

        def body(k, carry):
            i, device = peer(kind, jnp.where(k < late, k + farthest[kind], k - late + 1))
            pltpu.make_async_remote_copy(
                src_ref=source(i),
                dst_ref=target,
                send_sem=send_sem.at[step],
                recv_sem=recv_sem.at[step] if landed is None else landed,
                device_id=device,
                device_id_type=MESH,
            ).start()
            return carry

        lax.fori_loop(0, count[kind] - 1, body, 0)

    def arrived(step, ref):
        pltpu.make_async_copy(ref, ref, recv_sem.at[step]).wait()

    def id_arrived(i):
        pltpu.make_async_copy(ids.at[i], ids.at[i], ids_recv.at[i]).wait()

    def sent(step, ref):
        pltpu.make_async_copy(ref, ref, send_sem.at[step]).wait()

    loads = {
        name: pltpu.make_async_copy(source, target, load_sem.at[i])
        for i, (name, source, target) in enumerate(
            (
                ("c0", c0_in, c0_ref),
                ("pts", pts_in, pts_ref),
                ("cot", cot_in, cot_ref),
                ("c1", c1_in, c1_ref),
                ("c2", c2_in, c2_ref),
                ("nw", nw_in, nw_ref),
                ("src", src_in, src_ref),
                ("tiles", tiles_in, tiles_ref),
                ("halo", halo_in, halo_ref),
                ("up", up_in, up_ref),
                ("dn", dn_in, dn_ref),
            )
        )
    }
    barrier = pltpu.get_barrier_semaphore()

    reach = size_z // 4

    def greet(kind, steps, shift):
        def body(o, carry):
            _, device = peer(kind, o + shift)
            pl.semaphore_signal(barrier, inc=1, device_id=device, device_id_type=MESH)
            return carry

        lax.fori_loop(1, steps + 1, body, 0)

    greet("z", reach, 0)
    greet("z", reach, size_z - reach - 1)
    greet("q", size_q - 1, 0)
    beside = lax.rem(a + size_x - 1 + 2 * core, size_x)
    pl.semaphore_signal(barrier, inc=1, device_id=(beside, b), device_id_type=MESH)

    for load in loads.values():
        load.start()

    for name in ("c0", "pts", "cot", "c1", "c2"):
        loads[name].wait()
    points = pts_ref[...].reshape(PTS, C)
    cot = cot_ref[...]
    c0, c1, c2 = c0_ref[...], c1_ref[...], c2_ref[...]
    ot0[...] = one_hot_rows(c0, 0, OWN0 * size_y)
    ot1[...] = one_hot_rows(c1, 0, k1)
    ot2[...] = one_hot_rows(c2, 0, C)
    both = dot(ot0[...], jnp.concatenate([points, cot], axis=1))
    s_u0[...] = both[:, :C].astype(BF16)
    s_t0[...] = both[:, C:].astype(BF16)
    ids[b] = c0 * 1024 + c1
    lane = lax.broadcasted_iota(jnp.int32, (k2, C), 1)
    t2 = dot(ot2[...], cot)[:k2]
    s_p1[:, :C] = dot(ot1[...], cot).astype(BF16)
    counts = dot(ot1[...], ot2[...], NT)
    s_p1[2 * k2 :, C:] = counts[2 * k2 :].astype(BF16)
    s_p1[:k2, C:] = jnp.where(lane < k2, counts[:k2], pltpu.roll(t2, C - k2, 1)).astype(BF16)
    s_p1[k2 : 2 * k2, C:] = jnp.where(lane < k2, counts[k2 : 2 * k2], t2).astype(BF16)

    for name in ("nw", "src", "tiles", "halo", "up", "dn"):
        loads[name].wait()
    near_grad = dot(cot, nw_ref[...], NT).astype(BF16)
    returned = [jnp.zeros((BLK, C), F32)] * 4
    for t in range(4):
        rows = slice(t * BLK, (t + 1) * BLK)
        tile = tiles_ref[rows, :]
        sources = jnp.concatenate([pts_ref[src_ref[t, k]] for k in range(3)], axis=0)
        near[t] = dot(tile, sources)
        grad = near_grad[rows]
        pieces = dot(tile, grad, TN)
        for k in range(3):
            piece = pieces[k * BLK : (k + 1) * BLK]
            for s in range(4):
                returned[s] = returned[s] + jnp.where(src_ref[t, k] == s, piece, 0.0)
        spx[t] = dot(halo_ref[2 * t], grad, TN).astype(BF16)
        spy[t] = dot(halo_ref[2 * t + 1], grad, TN).astype(BF16)
    for s in range(4):
        ret[s] = returned[s]

    pl.semaphore_wait(barrier, 2 * reach + size_q - 1 + 1)
    for o in (reach, size_z - reach):
        _, device = peer("z", o)
        pl.semaphore_signal(relay, inc=1, device_id=device, device_id_type=MESH)

    exchange("y", 0, lambda i: ids.at[b], ids.at[b], ids_recv.at[b])
    exchange("y", 1, lambda i: s_u0.at[pl.ds(i * OWN0, OWN0)], r_u0.at[b])
    exchange("q", 2, lambda i: s_p1.at[pl.ds(i * 16, 16)], r_p1.at[q])
    has = (a > 0, a < size_x - 1, b > 0, b < size_y - 1)

    def halo_copies(side):
        if side == 0:
            return [[(pts_ref.at[pl.ds(0, 2)], fx.at[pl.ds(2, 2)])], [(spx.at[pl.ds(0, 2)], bx.at[pl.ds(2, 2)])]]
        if side == 1:
            return [[(pts_ref.at[pl.ds(2, 2)], fx.at[pl.ds(0, 2)])], [(spx.at[pl.ds(2, 2)], bx.at[pl.ds(0, 2)])]]
        if side == 2:
            return [[(pts_ref.at[i], fy.at[i + 1]) for i in (0, 2)], [(spy.at[i], by.at[i + 1]) for i in (0, 2)]]
        return [[(pts_ref.at[i], fy.at[i - 1]) for i in (1, 3)], [(spy.at[i], by.at[i - 1]) for i in (1, 3)]]

    neighbour = ((a - 1, b), (a + 1, b), (a, b - 1), (a, b + 1))
    landing = ((fx, bx, 0, 2), (fx, bx, 2, 4), (fy, by, 0, 2), (fy, by, 2, 4))
    edge = ((0, 1), (2, 3), (0, 2), (1, 3))

    def send_halo(kind, sides):
        for side in sides:

            @pl.when(has[side])
            def _(side=side):
                for source, target in halo_copies(side)[kind]:
                    pltpu.make_async_remote_copy(
                        src_ref=source,
                        dst_ref=target,
                        send_sem=halo_send.at[2 * side + kind],
                        recv_sem=halo_recv.at[2 * (side ^ 1) + kind],
                        device_id=neighbour[side],
                        device_id_type=MESH,
                    ).start()

    def wait_halo(kind):
        for side in range(4):
            ref = landing[side][kind]

            @pl.when(has[side])
            def _(side=side, ref=ref):
                two = ref.at[pl.ds(landing[side][2], 2)]
                pltpu.make_async_copy(two, two, halo_recv.at[2 * side + kind]).wait()

            @pl.when(jnp.logical_not(has[side]))
            def _(side=side, ref=ref):
                for i in edge[side]:
                    ref[i] = jnp.zeros((BLK, C), BF16)

    send_halo(0, (0, 1))
    send_halo(1, (0, 1))

    near_first = sorted(
        range(size_y),
        key=lambda o: min(o // side_x, side_y - o // side_x) + min(o % side_x, side_x - o % side_x),
    )
    fines = []
    pair_counts = jnp.zeros((OWN0, k1), F32)
    for n, o in enumerate(near_first):
        i = in_plane(o)
        if n > 0:
            id_arrived(i)
        packed = ids[i]
        fine = lax.shift_right_logical(packed, 10)
        mid = lax.bitwise_and(packed, 1023)
        fines.append(fine)
        here = slice(n * PTS, (n + 1) * PTS)
        cat1[:, here] = one_hot_rows(mid, 0, k1)
        pair_counts = pair_counts + dot(one_hot_rows(fine, b * OWN0, OWN0), cat1[:, here], NT)
    pair_counts = pair_counts.astype(BF16)

    def group_counts(first, last):
        for n in range(first, last):
            cat0[:, (n - first) * PTS : (n - first + 1) * PTS] = one_hot_rows(fines[n], 0, OWN0 * size_y)
        part = dot(cat0[:, : (last - first) * PTS], cat1[:, first * PTS : last * PTS], NT)
        if first == 0:
            group[...] = part
        else:
            group[...] += part

    r_u0[b] = s_u0[pl.ds(pl.multiple_of(b * OWN0, OWN0), OWN0), :]
    arrived(1, r_u0.at[pl.ds(0, size_y - 1)])
    u0 = jnp.sum(r_u0[...].astype(F32), axis=0)
    summed0 = dot_split(u0, up_ref[0])
    inverse0 = inverse_rms(summed0)
    normed0 = summed0 * inverse0
    n0 = normed0.astype(BF16)
    s_u1[...] = dot(pair_counts, n0, TN).astype(BF16)
    exchange("q", 4, lambda i: s_u1.at[pl.ds(i * 16, 16)], r_u1.at[q])
    mine32 = pl.ds(pl.multiple_of(b * OWN0, OWN0), OWN0)
    exchange("y", 3, lambda i: s_t0.at[pl.ds(i * OWN0, OWN0)], r_t0.at[b])

    mine16 = pl.ds(pl.multiple_of(q * 16, 16), 16)
    r_p1[q] = s_p1[mine16, :]
    arrived(2, r_p1.at[pl.ds(0, size_q - 1)])
    z_near, z_far = lax.rem(z, 4), lax.div(z, 4)
    n_p1[z_near] = jnp.sum(r_p1[...].astype(F32), axis=0).astype(BF16)
    pl.semaphore_wait(relay, 2)
    exchange("near", 6, lambda i: n_p1.at[z_near], n_p1.at[z_near])

    third = (size_y + 2) // 3
    group_counts(0, third)

    arrived(6, n_p1.at[pl.ds(0, 3)])
    f_p1[z_far] = jnp.sum(n_p1[...].astype(F32), axis=0).astype(BF16)
    exchange("far", 14, lambda i: f_p1.at[z_far], f_p1.at[z_far])

    r_u1[q] = s_u1[mine16, :]
    arrived(4, r_u1.at[pl.ds(0, size_q - 1)])
    z_u1[z] = jnp.sum(r_u1[...].astype(F32), axis=0).astype(BF16)
    exchange("z", 8, lambda i: z_u1.at[z], z_u1.at[z])

    r_t0[b] = s_t0[mine32, :]
    arrived(3, r_t0.at[pl.ds(0, size_y - 1)])
    t0 = jnp.sum(r_t0[...].astype(F32), axis=0)
    ut0[mine32, :C] = u0.astype(BF16)
    ut0[mine32, C:] = t0.astype(BF16)
    exchange("y", 5, lambda i: ut0.at[mine32], ut0.at[mine32])
    send_halo(0, (2, 3))
    group_counts(third, 2 * third)

    wait_halo(0)
    for t in range(4):
        total = near[t] + dot(halo_ref[2 * t], fx[t]) + dot(halo_ref[2 * t + 1], fy[t])
        nv[pl.ds(t * BLK, BLK), :] = total.astype(BF16)
    near_part = dot(nv[...], cot, TN)
    down0_part = dot(n0, t0.astype(BF16), TN)
    s_p2[...] = jnp.concatenate(
        [near_part.reshape(size_y, 8, C), down0_part.reshape(size_y, 8, C)], axis=1
    ).astype(BF16)
    exchange("q", 7, lambda i: s_p2.at[lax.rem(i, size_y)], r_p2.at[q])

    arrived(5, ut0.at[pl.ds(0, (size_y - 1) * OWN0)])
    u0_t[...] = ut0[:, :C].astype(F32).T.astype(BF16)
    summed0 = dot(ut0[:, :C], up_ref[0])
    inverse0 = inverse_rms(summed0)
    normed0 = summed0 * inverse0
    raw0 = dot(ut0[:, C:], dn_ref[0], NT)

    arrived(14, f_p1.at[pl.ds(0, size_z // 4 - 1)])
    p1[mine16, :] = jnp.sum(f_p1[...].astype(F32), axis=0).astype(BF16)
    exchange("q", 9, lambda i: p1.at[mine16], p1.at[mine16])

    arrived(8, z_u1.at[pl.ds(0, size_z - 1)])
    u1[mine16, :] = jnp.sum(z_u1[...].astype(F32), axis=0).astype(BF16)
    exchange("q", 11, lambda i: u1.at[mine16], u1.at[mine16])

    group_counts(2 * third, size_y)
    group_bf[...] = group[...].astype(BF16)
    combined = points.astype(F32) + dot(nv[...], nw_ref[...])
    combined = combined + dot(dot(ot0[...], normed0.astype(BF16), TN).astype(BF16), dn_ref[0])
    arrived(9, p1.at[pl.ds(0, (size_q - 1) * 16)])
    t1 = p1[:, :C]
    upper_part = p1[:k2, C:].astype(F32)
    t2 = jnp.where(lane < k2, pltpu.roll(upper_part, C - k2, 1), p1[k2 : 2 * k2, C:].astype(F32))
    t2 = t2.astype(BF16)
    counts = p1[:, C:][:, :k2]
    counts_t = counts.astype(F32).T.astype(BF16)

    r_p2[q] = s_p2[b]
    arrived(7, r_p2.at[pl.ds(0, size_q - 1)])
    z_p2[z] = jnp.sum(r_p2[...].astype(F32), axis=0).astype(BF16)
    exchange("z", 10, lambda i: z_p2.at[z], z_p2.at[z])

    raw2 = dot(t2, dn_ref[2], NT)
    raw1 = dot(t1, dn_ref[1], NT)
    arrived(11, u1.at[pl.ds(0, (size_q - 1) * 16)])
    summed1 = dot(u1[...], up_ref[1])
    inverse1 = inverse_rms(summed1)
    normed1 = summed1 * inverse1
    n1 = normed1.astype(BF16)
    u2 = dot(counts_t, n1)
    summed2 = dot_split(u2, up_ref[2])
    inverse2 = inverse_rms(summed2)
    normed2 = summed2 * inverse2
    n2 = normed2.astype(BF16)
    sg2 = norm_back(raw2, normed2, inverse2).astype(BF16)
    back2 = dot(sg2, up_ref[2], NT)
    back2_high = back2.astype(BF16)
    back2_low = (back2 - back2_high.astype(F32)).astype(BF16)
    raw1 = raw1 + dot(counts, back2_high) + dot(counts, back2_low)
    sg1 = norm_back(raw1, normed1, inverse1).astype(BF16)
    raw0 = raw0 + dot_split(dot(group_bf[...], sg1), up_ref[1], NT)
    sg0 = norm_back(raw0, normed0, inverse0).astype(BF16)
    s_d[...] = dot(u0_t[...], sg0).reshape(size_y, 8, C)
    to_pair = pltpu.make_async_remote_copy(
        src_ref=s_d.at[b],
        dst_ref=r_d,
        send_sem=send_sem.at[13],
        recv_sem=recv_sem.at[13],
        device_id=(a + 1 - 2 * core, b),
        device_id_type=MESH,
    )
    to_pair.start()

    wg_ref[2] = dot(u1[...], sg1, TN) * scale
    wg_ref[3] = dot_split(u2, sg2, TN) * scale
    to_pair.wait()
    z_d[z] = s_d[b] + r_d[...]
    exchange("z", 15, lambda i: z_d.at[z], z_d.at[z])
    send_halo(1, (2, 3))
    wg_ref[5] = dot(n1, t1, TN) * scale
    wg_ref[6] = dot(n2, t2, TN) * scale

    arrived(10, z_p2.at[pl.ds(0, size_z - 1)])
    g_p2[b] = jnp.sum(z_p2[...].astype(F32), axis=0) * scale
    exchange("y", 12, lambda i: g_p2.at[b], g_p2.at[b])

    combined = combined + dot(dot(ot1[...], n1, TN).astype(BF16), dn_ref[1])
    combined = combined + dot(dot(ot2[:k2, :], n2, TN).astype(BF16), dn_ref[2])
    mixed_ref[...] = combined.astype(BF16)
    put_mixed = pltpu.make_async_copy(mixed_ref, mixed_out, out_sem.at[0])
    put_mixed.start()

    wait_halo(1)
    for t in range(4):
        ret[t] = ret[t] + bx[t].astype(F32) + by[t].astype(F32)
    upper0 = dot(ot0[...], sg0, TN).astype(BF16)
    grad = cot.astype(F32) + ret[...].reshape(PTS, C) + dot(upper0, up_ref[0], NT)
    pg_ref[...] = grad.astype(BF16)
    put_pg = pltpu.make_async_copy(pg_ref, pg_out, out_sem.at[1])
    put_pg.start()

    arrived(12, g_p2.at[pl.ds(0, size_y - 1)])
    wg_ref[0] = g_p2[:, :8, :].reshape(C, C)
    wg_ref[4] = g_p2[:, 8:, :].reshape(C, C)
    put_first = pltpu.make_async_copy(wg_ref.at[0], wg_out.at[0], out_sem.at[2])
    put_first.start()
    put_rest = pltpu.make_async_copy(wg_ref.at[pl.ds(2, 5)], wg_out.at[pl.ds(2, 5)], out_sem.at[3])
    put_rest.start()

    arrived(15, z_d.at[pl.ds(0, size_z - 1)])
    mine8 = pl.ds(pl.multiple_of(b * 8, 8), 8)
    wg_ref[1, mine8, :] = jnp.sum(z_d[...], axis=0) * scale
    exchange("y", 16, lambda i: wg_ref.at[1, mine8], wg_out.at[1, mine8])
    put_last = pltpu.make_async_copy(wg_ref.at[1, mine8], wg_out.at[1, mine8], out_sem.at[4])
    put_last.start()
    for step, ref in (
        (0, ids.at[pl.ds(0, size_y - 1)]),
        (1, r_u0.at[pl.ds(0, size_y - 1)]),
        (2, r_p1.at[pl.ds(0, size_q - 1)]),
        (3, r_t0.at[pl.ds(0, size_y - 1)]),
        (4, r_u1.at[pl.ds(0, size_q - 1)]),
        (5, ut0.at[pl.ds(0, (size_y - 1) * OWN0)]),
        (6, n_p1.at[pl.ds(0, 3)]),
        (14, f_p1.at[pl.ds(0, size_z // 4 - 1)]),
        (7, r_p2.at[pl.ds(0, size_q - 1)]),
        (8, z_u1.at[pl.ds(0, size_z - 1)]),
        (9, p1.at[pl.ds(0, (size_q - 1) * 16)]),
        (10, z_p2.at[pl.ds(0, size_z - 1)]),
        (11, u1.at[pl.ds(0, (size_q - 1) * 16)]),
        (12, g_p2.at[pl.ds(0, size_y - 1)]),
        (15, z_d.at[pl.ds(0, size_z - 1)]),
    ):
        sent(step, ref)
    for side in range(4):

        @pl.when(has[side])
        def _(side=side):
            for kind in range(2):
                two = fx.at[pl.ds(0, 2)]
                pltpu.make_async_copy(two, two, halo_send.at[2 * side + kind]).wait()

    for put in (put_mixed, put_pg, put_first, put_rest, put_last):
        put.wait()
    arrived(16, wg_out.at[1, pl.ds(0, (size_y - 1) * 8)])
    sent(16, wg_out.at[1, pl.ds(0, (size_y - 1) * 8)])


def store(*refs):
    sources, targets, held, sem = refs[:3], refs[3:6], refs[6:9], refs[9]
    parts = [(2, pl.ds(i, 1)) for i in range(7)]
    parts += [(n, pl.ds(i * BLK, BLK)) for n in (0, 1) for i in range(PTS // BLK)]
    first, then = [], []
    for p, (n, part) in enumerate(parts):
        first.append(pltpu.make_async_copy(sources[n].at[part], held[n].at[part], sem.at[0, p]))
        then.append(pltpu.make_async_copy(held[n].at[part], targets[n].at[part], sem.at[1, p]))
    for copy in first:
        copy.start()
    for p in range(len(parts)):
        first[p].wait()
        then[p].start()
    for copy in then:
        copy.wait()


def on_device(
    size_x,
    size_y,
    points,
    cotangent,
    local_tiles,
    local_source,
    halo_tiles,
    cluster_fine,
    cluster_mid,
    cluster_coarse,
    near_weight,
    up_weights,
    down_weights,
):
    size_z, size_q, k1 = size_x // 2, 2 * size_y, size_x * size_y
    k0 = OWN0 * size_y
    blocks = pltpu.VMEM((4, BLK, C), BF16)
    hbm = pl.BlockSpec(memory_space=pltpu.HBM)
    scratch = [
        pltpu.VMEM((PTS, C), BF16),
        pltpu.VMEM((PTS, C), BF16),
        pltpu.VMEM((7, C, C), F32),
        pltpu.SemaphoreType.DMA((5,)),
        pltpu.VMEM((4, BLK, C), BF16),
        pltpu.VMEM((PTS, C), BF16),
        pltpu.VMEM((PTS, 3 * BLK), BF16),
        pltpu.SMEM((4, 3), jnp.int32),
        pltpu.VMEM((8, BLK, BLK), BF16),
        pltpu.VMEM((1, PTS), jnp.int32),
        pltpu.VMEM((1, PTS), jnp.int32),
        pltpu.VMEM((1, PTS), jnp.int32),
        pltpu.VMEM((C, C), BF16),
        pltpu.VMEM((3, C, C), BF16),
        pltpu.VMEM((3, C, C), BF16),
        pltpu.SemaphoreType.DMA((11,)),
        pltpu.VMEM((k0, PTS), BF16),
        pltpu.VMEM((k1, PTS), BF16),
        pltpu.VMEM((C, PTS), BF16),
        pltpu.VMEM((4, BLK, C), F32),
        pltpu.VMEM((4, BLK, C), F32),
        pltpu.VMEM((PTS, C), BF16),
        blocks,
        blocks,
        blocks,
        blocks,
        blocks,
        blocks,
        pltpu.VMEM((size_y, 1, PTS), jnp.int32),
        pltpu.VMEM((k0, C), BF16),
        pltpu.VMEM((size_y, OWN0, C), BF16),
        pltpu.VMEM((k0, C), BF16),
        pltpu.VMEM((size_y, OWN0, C), BF16),
        pltpu.VMEM((k1, 2 * C), BF16),
        pltpu.VMEM((size_q, 16, 2 * C), BF16),
        pltpu.VMEM((4, 16, 2 * C), BF16),
        pltpu.VMEM((size_z // 4, 16, 2 * C), BF16),
        pltpu.VMEM((k1, 2 * C), BF16),
        pltpu.VMEM((k1, C), BF16),
        pltpu.VMEM((size_q, 16, C), BF16),
        pltpu.VMEM((size_z, 16, C), BF16),
        pltpu.VMEM((k1, C), BF16),
        pltpu.VMEM((k0, 2 * C), BF16),
        pltpu.VMEM((C, k0), BF16),
        pltpu.VMEM((k0, (size_y + 2) // 3 * PTS), BF16),
        pltpu.VMEM((k1, size_y * PTS), BF16),
        pltpu.VMEM((k0, k1), F32),
        pltpu.VMEM((k0, k1), BF16),
        pltpu.VMEM((size_y, 16, C), BF16),
        pltpu.VMEM((size_q, 16, C), BF16),
        pltpu.VMEM((size_z, 16, C), BF16),
        pltpu.VMEM((size_y, 16, C), F32),
        pltpu.VMEM((size_y, 8, C), F32),
        pltpu.VMEM((8, C), F32),
        pltpu.VMEM((size_z, 8, C), F32),
        pltpu.SemaphoreType.DMA((17,)),
        pltpu.SemaphoreType.DMA((17,)),
        pltpu.SemaphoreType.DMA((8,)),
        pltpu.SemaphoreType.DMA((8,)),
        pltpu.SemaphoreType.DMA((size_y,)),
        pltpu.SemaphoreType.REGULAR,
    ]
    outs = pl.pallas_call(
        functools.partial(kernel, size_x, size_y),
        out_shape=(
            jax.ShapeDtypeStruct((PTS, C), BF16),
            jax.ShapeDtypeStruct((PTS, C), BF16),
            jax.ShapeDtypeStruct((7, C, C), F32),
        ),
        in_specs=[hbm] * 11,
        out_specs=(hbm,) * 3,
        scratch_shapes=scratch,
        name="layer",
        compiler_params=pltpu.CompilerParams(
            collective_id=0, has_side_effects=True, vmem_limit_bytes=60 * 1024 * 1024
        ),
    )(
        points.reshape(4, BLK, C),
        cotangent,
        local_tiles,
        local_source,
        halo_tiles.reshape(8, BLK, BLK),
        cluster_fine.reshape(1, PTS),
        cluster_mid.reshape(1, PTS),
        cluster_coarse.reshape(1, PTS),
        near_weight,
        up_weights,
        down_weights,
    )
    return pl.pallas_call(
        store,
        out_shape=tuple(jax.ShapeDtypeStruct(o.shape, o.dtype) for o in outs),
        in_specs=[hbm] * 3,
        out_specs=(hbm,) * 3,
        scratch_shapes=[pltpu.VMEM(o.shape, o.dtype) for o in outs] + [pltpu.SemaphoreType.DMA((2, 15))],
        name="store",
        compiler_params=pltpu.CompilerParams(vmem_limit_bytes=60 * 1024 * 1024),
    )(*outs)


def solution(mesh):
    rows = P(("gx", "gy"), None)
    flat = P(("gx", "gy"))
    size_x, size_y = mesh.shape["gx"], mesh.shape["gy"]
    return jax.shard_map(
        functools.partial(on_device, size_x, size_y),
        mesh=mesh,
        in_specs=(rows, rows, rows, rows, rows, flat, flat, flat, P(), P(), P()),
        out_specs=(rows, rows, P()),
        check_vma=False,
    )
```

```python
import functools
import math

import jax
import jax.numpy as jnp
from jax import lax
from jax.experimental import pallas as pl
from jax.experimental.pallas import tpu as pltpu
from jax.sharding import PartitionSpec as P

BLK = 128
C = 128
PTS = 512
OWN0 = 32
EPSILON = 1e-05
MESH = pl.DeviceIdType.MESH
F32, BF16 = jnp.float32, jnp.bfloat16

NN = ((1,), (0,))
NT = ((1,), (1,))
TN = ((0,), (0,))


def dot(a, b, dims=NN):
    return lax.dot_general(a, b, (dims, ((), ())), preferred_element_type=F32)


def dot_split(a, b, dims=NN):
    high = a.astype(BF16)
    low = (a - high.astype(F32)).astype(BF16)
    (left,), (right,) = dims
    return dot(
        jnp.concatenate([high, low], axis=left), jnp.concatenate([b, b], axis=right), dims
    )


def one_hot_rows(ids, first, count):
    rows = lax.broadcasted_iota(jnp.int32, (count, ids.shape[1]), 0) + first
    return jnp.where(rows == ids, 1.0, 0.0).astype(BF16)


def inverse_rms(summed):
    return lax.rsqrt(jnp.mean(summed * summed, axis=-1, keepdims=True) + EPSILON)


def norm_back(raw, normed, inverse):
    return inverse * (raw - normed * jnp.mean(raw * normed, axis=-1, keepdims=True))


def kernel(
    size_x,
    size_y,
    pts_in,
    cot_in,
    tiles_in,
    src_in,
    halo_in,
    c0_in,
    c1_in,
    c2_in,
    nw_in,
    up_in,
    dn_in,
    mixed_out,
    pg_out,
    wg_out,
    mixed_ref,
    pg_ref,
    wg_ref,
    out_sem,
    pts_ref,
    cot_ref,
    tiles_ref,
    src_ref,
    halo_ref,
    c0_ref,
    c1_ref,
    c2_ref,
    nw_ref,
    up_ref,
    dn_ref,
    load_sem,
    ot0,
    ot1,
    ot2,
    near,
    ret,
    nv,
    spx,
    spy,
    fx,
    fy,
    bx,
    by,
    ids,
    s_u0,
    r_u0,
    s_t0,
    r_t0,
    s_p1,
    r_p1,
    n_p1,
    f_p1,
    p1,
    s_u1,
    r_u1,
    z_u1,
    u1,
    ut0,
    u0_t,
    cat0,
    cat1,
    group,
    group_bf,
    s_p2,
    r_p2,
    z_p2,
    g_p2,
    s_d,
    r_d,
    z_d,
    send_sem,
    recv_sem,
    halo_send,
    halo_recv,
    ids_recv,
    relay,
):
    size_z = size_x // 2
    size_q = 2 * size_y
    k1 = size_x * size_y
    k2 = k1 // 8
    a = lax.axis_index("gx")
    b = lax.axis_index("gy")
    z = lax.div(a, 2)
    core = lax.rem(a, 2)
    q = core * size_y + b
    scale = 1.0 / math.sqrt(PTS * size_x * size_y)

    side_y = math.isqrt(size_y)
    side_x = size_y // side_y

    def in_plane(o):
        x = lax.rem(lax.div(b, side_x) + lax.div(o, side_x), side_y)
        return x * side_x + lax.rem(lax.rem(b, side_x) + lax.rem(o, side_x), side_x)

    def peer(kind, o):
        if kind == "y":
            i = in_plane(o)
            return i, (a, i)
        if kind == "z":
            i = lax.rem(z + o, size_z)
            return i, (i * 2 + core, b)
        if kind == "near":
            i = lax.rem(z + o, 4)
            return i, ((z - lax.rem(z, 4) + i) * 2 + core, b)
        if kind == "far":
            i = lax.rem(z + 4 * o, size_z)
            return lax.div(i, 4), (i * 2 + core, b)
        c = lax.rem(core + o, 2)
        i = in_plane(lax.div(o, 2))
        return c * size_y + i, (z * 2 + c, i)

    farthest = {
        "y": size_y // 2 + side_x // 2,
        "z": size_z // 2,
        "q": size_y + 2 * (side_x // 2),
        "near": 2,
        "far": size_z // 8,
    }
    count = {"y": size_y, "z": size_z, "q": size_q, "near": 4, "far": size_z // 4}

    def exchange(kind, step, source, target, landed=None):
        late = count[kind] - farthest[kind]

        def body(k, carry):
            i, device = peer(kind, jnp.where(k < late, k + farthest[kind], k - late + 1))
            pltpu.make_async_remote_copy(
                src_ref=source(i),
                dst_ref=target,
                send_sem=send_sem.at[step],
                recv_sem=recv_sem.at[step] if landed is None else landed,
                device_id=device,
                device_id_type=MESH,
            ).start()
            return carry

        lax.fori_loop(0, count[kind] - 1, body, 0)

    def arrived(step, ref):
        pltpu.make_async_copy(ref, ref, recv_sem.at[step]).wait()

    def id_arrived(i):
        pltpu.make_async_copy(ids.at[i], ids.at[i], ids_recv.at[i]).wait()

    def sent(step, ref):
        pltpu.make_async_copy(ref, ref, send_sem.at[step]).wait()

    loads = {
        name: pltpu.make_async_copy(source, target, load_sem.at[i])
        for i, (name, source, target) in enumerate(
            (
                ("c0", c0_in, c0_ref),
                ("pts", pts_in, pts_ref),
                ("cot", cot_in, cot_ref),
                ("c1", c1_in, c1_ref),
                ("c2", c2_in, c2_ref),
                ("nw", nw_in, nw_ref),
                ("src", src_in, src_ref),
                ("tiles", tiles_in, tiles_ref),
                ("halo", halo_in, halo_ref),
                ("up", up_in, up_ref),
                ("dn", dn_in, dn_ref),
            )
        )
    }
    barrier = pltpu.get_barrier_semaphore()

    reach = size_z // 4

    def greet(kind, steps, shift):
        def body(o, carry):
            _, device = peer(kind, o + shift)
            pl.semaphore_signal(barrier, inc=1, device_id=device, device_id_type=MESH)
            return carry

        lax.fori_loop(1, steps + 1, body, 0)

    greet("z", reach, 0)
    greet("z", reach, size_z - reach - 1)
    greet("q", size_q - 1, 0)
    beside = lax.rem(a + size_x - 1 + 2 * core, size_x)
    pl.semaphore_signal(barrier, inc=1, device_id=(beside, b), device_id_type=MESH)

    for load in loads.values():
        load.start()

    for name in ("c0", "pts", "cot", "c1", "c2"):
        loads[name].wait()
    points = pts_ref[...].reshape(PTS, C)
    cot = cot_ref[...]
    c0, c1, c2 = c0_ref[...], c1_ref[...], c2_ref[...]
    ot0[...] = one_hot_rows(c0, 0, OWN0 * size_y)
    ot1[...] = one_hot_rows(c1, 0, k1)
    ot2[...] = one_hot_rows(c2, 0, C)
    both = dot(ot0[...], jnp.concatenate([points, cot], axis=1))
    s_u0[...] = both[:, :C].astype(BF16)
    s_t0[...] = both[:, C:].astype(BF16)
    ids[b] = c0 * 1024 + c1
    lane = lax.broadcasted_iota(jnp.int32, (k2, C), 1)
    t2 = dot(ot2[...], cot)[:k2]
    s_p1[:, :C] = dot(ot1[...], cot).astype(BF16)
    counts = dot(ot1[...], ot2[...], NT)
    s_p1[2 * k2 :, C:] = counts[2 * k2 :].astype(BF16)
    s_p1[:k2, C:] = jnp.where(lane < k2, counts[:k2], pltpu.roll(t2, C - k2, 1)).astype(BF16)
    s_p1[k2 : 2 * k2, C:] = jnp.where(lane < k2, counts[k2 : 2 * k2], t2).astype(BF16)

    for name in ("nw", "src", "tiles", "halo", "up", "dn"):
        loads[name].wait()
    near_grad = dot(cot, nw_ref[...], NT).astype(BF16)
    returned = [jnp.zeros((BLK, C), F32)] * 4
    for t in range(4):
        rows = slice(t * BLK, (t + 1) * BLK)
        tile = tiles_ref[rows, :]
        sources = jnp.concatenate([pts_ref[src_ref[t, k]] for k in range(3)], axis=0)
        near[t] = dot(tile, sources)
        grad = near_grad[rows]
        pieces = dot(tile, grad, TN)
        for k in range(3):
            piece = pieces[k * BLK : (k + 1) * BLK]
            for s in range(4):
                returned[s] = returned[s] + jnp.where(src_ref[t, k] == s, piece, 0.0)
        spx[t] = dot(halo_ref[2 * t], grad, TN).astype(BF16)
        spy[t] = dot(halo_ref[2 * t + 1], grad, TN).astype(BF16)
    for s in range(4):
        ret[s] = returned[s]

    pl.semaphore_wait(barrier, 2 * reach + size_q - 1 + 1)
    for o in (reach, size_z - reach):
        _, device = peer("z", o)
        pl.semaphore_signal(relay, inc=1, device_id=device, device_id_type=MESH)

    exchange("y", 0, lambda i: ids.at[b], ids.at[b], ids_recv.at[b])
    exchange("y", 1, lambda i: s_u0.at[pl.ds(i * OWN0, OWN0)], r_u0.at[b])
    exchange("q", 2, lambda i: s_p1.at[pl.ds(i * 16, 16)], r_p1.at[q])
    has = (a > 0, a < size_x - 1, b > 0, b < size_y - 1)

    def halo_copies(side):
        if side == 0:
            return [[(pts_ref.at[pl.ds(0, 2)], fx.at[pl.ds(2, 2)])], [(spx.at[pl.ds(0, 2)], bx.at[pl.ds(2, 2)])]]
        if side == 1:
            return [[(pts_ref.at[pl.ds(2, 2)], fx.at[pl.ds(0, 2)])], [(spx.at[pl.ds(2, 2)], bx.at[pl.ds(0, 2)])]]
        if side == 2:
            return [[(pts_ref.at[i], fy.at[i + 1]) for i in (0, 2)], [(spy.at[i], by.at[i + 1]) for i in (0, 2)]]
        return [[(pts_ref.at[i], fy.at[i - 1]) for i in (1, 3)], [(spy.at[i], by.at[i - 1]) for i in (1, 3)]]

    neighbour = ((a - 1, b), (a + 1, b), (a, b - 1), (a, b + 1))
    landing = ((fx, bx, 0, 2), (fx, bx, 2, 4), (fy, by, 0, 2), (fy, by, 2, 4))
    edge = ((0, 1), (2, 3), (0, 2), (1, 3))

    def send_halo(kind, sides):
        for side in sides:

            @pl.when(has[side])
            def _(side=side):
                for source, target in halo_copies(side)[kind]:
                    pltpu.make_async_remote_copy(
                        src_ref=source,
                        dst_ref=target,
                        send_sem=halo_send.at[2 * side + kind],
                        recv_sem=halo_recv.at[2 * (side ^ 1) + kind],
                        device_id=neighbour[side],
                        device_id_type=MESH,
                    ).start()

    def wait_halo(kind):
        for side in range(4):
            ref = landing[side][kind]

            @pl.when(has[side])
            def _(side=side, ref=ref):
                two = ref.at[pl.ds(landing[side][2], 2)]
                pltpu.make_async_copy(two, two, halo_recv.at[2 * side + kind]).wait()

            @pl.when(jnp.logical_not(has[side]))
            def _(side=side, ref=ref):
                for i in edge[side]:
                    ref[i] = jnp.zeros((BLK, C), BF16)

    send_halo(0, (0, 1))
    send_halo(1, (0, 1))

    near_first = sorted(
        range(size_y),
        key=lambda o: min(o // side_x, side_y - o // side_x) + min(o % side_x, side_x - o % side_x),
    )
    fines = []
    pair_counts = jnp.zeros((OWN0, k1), F32)
    for n, o in enumerate(near_first):
        i = in_plane(o)
        if n > 0:
            id_arrived(i)
        packed = ids[i]
        fine = lax.shift_right_logical(packed, 10)
        mid = lax.bitwise_and(packed, 1023)
        fines.append(fine)
        here = slice(n * PTS, (n + 1) * PTS)
        cat1[:, here] = one_hot_rows(mid, 0, k1)
        pair_counts = pair_counts + dot(one_hot_rows(fine, b * OWN0, OWN0), cat1[:, here], NT)
    pair_counts = pair_counts.astype(BF16)

    def group_counts(first, last):
        for n in range(first, last):
            cat0[:, (n - first) * PTS : (n - first + 1) * PTS] = one_hot_rows(fines[n], 0, OWN0 * size_y)
        part = dot(cat0[:, : (last - first) * PTS], cat1[:, first * PTS : last * PTS], NT)
        if first == 0:
            group[...] = part
        else:
            group[...] += part

    r_u0[b] = s_u0[pl.ds(pl.multiple_of(b * OWN0, OWN0), OWN0), :]
    arrived(1, r_u0.at[pl.ds(0, size_y - 1)])
    u0 = jnp.sum(r_u0[...].astype(F32), axis=0)
    summed0 = dot_split(u0, up_ref[0])
    inverse0 = inverse_rms(summed0)
    normed0 = summed0 * inverse0
    n0 = normed0.astype(BF16)
    s_u1[...] = dot(pair_counts, n0, TN).astype(BF16)
    exchange("q", 4, lambda i: s_u1.at[pl.ds(i * 16, 16)], r_u1.at[q])
    mine32 = pl.ds(pl.multiple_of(b * OWN0, OWN0), OWN0)
    exchange("y", 3, lambda i: s_t0.at[pl.ds(i * OWN0, OWN0)], r_t0.at[b])

    mine16 = pl.ds(pl.multiple_of(q * 16, 16), 16)
    r_p1[q] = s_p1[mine16, :]
    arrived(2, r_p1.at[pl.ds(0, size_q - 1)])
    z_near, z_far = lax.rem(z, 4), lax.div(z, 4)
    n_p1[z_near] = jnp.sum(r_p1[...].astype(F32), axis=0).astype(BF16)
    pl.semaphore_wait(relay, 2)
    exchange("near", 6, lambda i: n_p1.at[z_near], n_p1.at[z_near])

    third = (size_y + 2) // 3
    group_counts(0, third)

    arrived(6, n_p1.at[pl.ds(0, 3)])
    f_p1[z_far] = jnp.sum(n_p1[...].astype(F32), axis=0).astype(BF16)
    exchange("far", 14, lambda i: f_p1.at[z_far], f_p1.at[z_far])

    r_u1[q] = s_u1[mine16, :]
    arrived(4, r_u1.at[pl.ds(0, size_q - 1)])
    z_u1[z] = jnp.sum(r_u1[...].astype(F32), axis=0).astype(BF16)
    exchange("z", 8, lambda i: z_u1.at[z], z_u1.at[z])

    r_t0[b] = s_t0[mine32, :]
    arrived(3, r_t0.at[pl.ds(0, size_y - 1)])
    t0 = jnp.sum(r_t0[...].astype(F32), axis=0)
    ut0[mine32, :C] = u0.astype(BF16)
    ut0[mine32, C:] = t0.astype(BF16)
    exchange("y", 5, lambda i: ut0.at[mine32], ut0.at[mine32])
    send_halo(0, (2, 3))
    group_counts(third, 2 * third)

    wait_halo(0)
    for t in range(4):
        total = near[t] + dot(halo_ref[2 * t], fx[t]) + dot(halo_ref[2 * t + 1], fy[t])
        nv[pl.ds(t * BLK, BLK), :] = total.astype(BF16)
    near_part = dot(nv[...], cot, TN)
    down0_part = dot(n0, t0.astype(BF16), TN)
    s_p2[...] = jnp.concatenate(
        [near_part.reshape(size_y, 8, C), down0_part.reshape(size_y, 8, C)], axis=1
    ).astype(BF16)
    exchange("q", 7, lambda i: s_p2.at[lax.rem(i, size_y)], r_p2.at[q])

    arrived(5, ut0.at[pl.ds(0, (size_y - 1) * OWN0)])
    u0_t[...] = ut0[:, :C].astype(F32).T.astype(BF16)
    summed0 = dot(ut0[:, :C], up_ref[0])
    inverse0 = inverse_rms(summed0)
    normed0 = summed0 * inverse0
    raw0 = dot(ut0[:, C:], dn_ref[0], NT)

    arrived(14, f_p1.at[pl.ds(0, size_z // 4 - 1)])
    p1[mine16, :] = jnp.sum(f_p1[...].astype(F32), axis=0).astype(BF16)
    exchange("q", 9, lambda i: p1.at[mine16], p1.at[mine16])

    arrived(8, z_u1.at[pl.ds(0, size_z - 1)])
    u1[mine16, :] = jnp.sum(z_u1[...].astype(F32), axis=0).astype(BF16)
    exchange("q", 11, lambda i: u1.at[mine16], u1.at[mine16])

    group_counts(2 * third, size_y)
    group_bf[...] = group[...].astype(BF16)
    combined = points.astype(F32) + dot(nv[...], nw_ref[...])
    combined = combined + dot(dot(ot0[...], normed0.astype(BF16), TN).astype(BF16), dn_ref[0])
    arrived(9, p1.at[pl.ds(0, (size_q - 1) * 16)])
    t1 = p1[:, :C]
    upper_part = p1[:k2, C:].astype(F32)
    t2 = jnp.where(lane < k2, pltpu.roll(upper_part, C - k2, 1), p1[k2 : 2 * k2, C:].astype(F32))
    t2 = t2.astype(BF16)
    counts = p1[:, C:][:, :k2]
    counts_t = counts.astype(F32).T.astype(BF16)
    wide = p1[:, C:].astype(F32)
    half = lax.broadcasted_iota(jnp.int32, (k1, C), 1) < k2
    counts_twice = jnp.where(half, wide, pltpu.roll(wide, k2, 1)).astype(BF16)

    r_p2[q] = s_p2[b]
    arrived(7, r_p2.at[pl.ds(0, size_q - 1)])
    z_p2[z] = jnp.sum(r_p2[...].astype(F32), axis=0).astype(BF16)
    exchange("z", 10, lambda i: z_p2.at[z], z_p2.at[z])

    raw2 = dot(t2, dn_ref[2], NT)
    raw1 = dot(t1, dn_ref[1], NT)
    arrived(11, u1.at[pl.ds(0, (size_q - 1) * 16)])
    summed1 = dot(u1[...], up_ref[1])
    inverse1 = inverse_rms(summed1)
    normed1 = summed1 * inverse1
    n1 = normed1.astype(BF16)
    u2 = dot(counts_t, n1)
    summed2 = dot_split(u2, up_ref[2])
    inverse2 = inverse_rms(summed2)
    normed2 = summed2 * inverse2
    n2 = normed2.astype(BF16)
    sg2 = norm_back(raw2, normed2, inverse2).astype(BF16)
    back2 = dot(sg2, up_ref[2], NT)
    back2_high = back2.astype(BF16)
    back2_low = (back2 - back2_high.astype(F32)).astype(BF16)
    raw1 = raw1 + dot(counts_twice, jnp.concatenate([back2_high, back2_low], axis=0))
    sg1 = norm_back(raw1, normed1, inverse1).astype(BF16)
    raw0 = raw0 + dot_split(dot(group_bf[...], sg1), up_ref[1], NT)
    sg0 = norm_back(raw0, normed0, inverse0).astype(BF16)
    s_d[...] = dot(u0_t[...], sg0).reshape(size_y, 8, C)
    to_pair = pltpu.make_async_remote_copy(
        src_ref=s_d.at[b],
        dst_ref=r_d,
        send_sem=send_sem.at[13],
        recv_sem=recv_sem.at[13],
        device_id=(a + 1 - 2 * core, b),
        device_id_type=MESH,
    )
    to_pair.start()

    wg_ref[2] = dot(u1[...], sg1, TN) * scale
    wg_ref[3] = dot_split(u2, sg2, TN) * scale
    to_pair.wait()
    z_d[z] = s_d[b] + r_d[...]
    exchange("z", 15, lambda i: z_d.at[z], z_d.at[z])
    send_halo(1, (2, 3))
    wg_ref[5] = dot(n1, t1, TN) * scale
    wg_ref[6] = dot(n2, t2, TN) * scale

    arrived(10, z_p2.at[pl.ds(0, size_z - 1)])
    g_p2[b] = jnp.sum(z_p2[...].astype(F32), axis=0) * scale
    exchange("y", 12, lambda i: g_p2.at[b], g_p2.at[b])

    combined = combined + dot(dot(ot1[...], n1, TN).astype(BF16), dn_ref[1])
    combined = combined + dot(dot(ot2[:k2, :], n2, TN).astype(BF16), dn_ref[2])
    mixed_ref[...] = combined.astype(BF16)
    put_mixed = pltpu.make_async_copy(mixed_ref, mixed_out, out_sem.at[0])
    put_mixed.start()

    wait_halo(1)
    for t in range(4):
        ret[t] = ret[t] + bx[t].astype(F32) + by[t].astype(F32)
    upper0 = dot(ot0[...], sg0, TN).astype(BF16)
    grad = cot.astype(F32) + ret[...].reshape(PTS, C) + dot(upper0, up_ref[0], NT)
    pg_ref[...] = grad.astype(BF16)
    put_pg = pltpu.make_async_copy(pg_ref, pg_out, out_sem.at[1])
    put_pg.start()

    arrived(12, g_p2.at[pl.ds(0, size_y - 1)])
    wg_ref[0] = g_p2[:, :8, :].reshape(C, C)
    wg_ref[4] = g_p2[:, 8:, :].reshape(C, C)
    put_first = pltpu.make_async_copy(wg_ref.at[0], wg_out.at[0], out_sem.at[2])
    put_first.start()
    put_rest = pltpu.make_async_copy(wg_ref.at[pl.ds(2, 5)], wg_out.at[pl.ds(2, 5)], out_sem.at[3])
    put_rest.start()

    arrived(15, z_d.at[pl.ds(0, size_z - 1)])
    mine8 = pl.ds(pl.multiple_of(b * 8, 8), 8)
    wg_ref[1, mine8, :] = jnp.sum(z_d[...], axis=0) * scale
    exchange("y", 16, lambda i: wg_ref.at[1, mine8], wg_out.at[1, mine8])
    put_last = pltpu.make_async_copy(wg_ref.at[1, mine8], wg_out.at[1, mine8], out_sem.at[4])
    put_last.start()
    for step, ref in (
        (0, ids.at[pl.ds(0, size_y - 1)]),
        (1, r_u0.at[pl.ds(0, size_y - 1)]),
        (2, r_p1.at[pl.ds(0, size_q - 1)]),
        (3, r_t0.at[pl.ds(0, size_y - 1)]),
        (4, r_u1.at[pl.ds(0, size_q - 1)]),
        (5, ut0.at[pl.ds(0, (size_y - 1) * OWN0)]),
        (6, n_p1.at[pl.ds(0, 3)]),
        (14, f_p1.at[pl.ds(0, size_z // 4 - 1)]),
        (7, r_p2.at[pl.ds(0, size_q - 1)]),
        (8, z_u1.at[pl.ds(0, size_z - 1)]),
        (9, p1.at[pl.ds(0, (size_q - 1) * 16)]),
        (10, z_p2.at[pl.ds(0, size_z - 1)]),
        (11, u1.at[pl.ds(0, (size_q - 1) * 16)]),
        (12, g_p2.at[pl.ds(0, size_y - 1)]),
        (15, z_d.at[pl.ds(0, size_z - 1)]),
    ):
        sent(step, ref)
    for side in range(4):

        @pl.when(has[side])
        def _(side=side):
            for kind in range(2):
                two = fx.at[pl.ds(0, 2)]
                pltpu.make_async_copy(two, two, halo_send.at[2 * side + kind]).wait()

    for put in (put_mixed, put_pg, put_first, put_rest, put_last):
        put.wait()
    arrived(16, wg_out.at[1, pl.ds(0, (size_y - 1) * 8)])
    sent(16, wg_out.at[1, pl.ds(0, (size_y - 1) * 8)])


def store(*refs):
    sources, targets, held, sem = refs[:3], refs[3:6], refs[6:9], refs[9]
    parts = [(2, pl.ds(i, 1)) for i in range(7)]
    parts += [(n, pl.ds(i * BLK, BLK)) for n in (0, 1) for i in range(PTS // BLK)]
    first, then = [], []
    for p, (n, part) in enumerate(parts):
        first.append(pltpu.make_async_copy(sources[n].at[part], held[n].at[part], sem.at[0, p]))
        then.append(pltpu.make_async_copy(held[n].at[part], targets[n].at[part], sem.at[1, p]))
    for copy in first:
        copy.start()
    for p in range(len(parts)):
        first[p].wait()
        then[p].start()
    for copy in then:
        copy.wait()


def on_device(
    size_x,
    size_y,
    points,
    cotangent,
    local_tiles,
    local_source,
    halo_tiles,
    cluster_fine,
    cluster_mid,
    cluster_coarse,
    near_weight,
    up_weights,
    down_weights,
):
    size_z, size_q, k1 = size_x // 2, 2 * size_y, size_x * size_y
    k0 = OWN0 * size_y
    blocks = pltpu.VMEM((4, BLK, C), BF16)
    hbm = pl.BlockSpec(memory_space=pltpu.HBM)
    scratch = [
        pltpu.VMEM((PTS, C), BF16),
        pltpu.VMEM((PTS, C), BF16),
        pltpu.VMEM((7, C, C), F32),
        pltpu.SemaphoreType.DMA((5,)),
        pltpu.VMEM((4, BLK, C), BF16),
        pltpu.VMEM((PTS, C), BF16),
        pltpu.VMEM((PTS, 3 * BLK), BF16),
        pltpu.SMEM((4, 3), jnp.int32),
        pltpu.VMEM((8, BLK, BLK), BF16),
        pltpu.VMEM((1, PTS), jnp.int32),
        pltpu.VMEM((1, PTS), jnp.int32),
        pltpu.VMEM((1, PTS), jnp.int32),
        pltpu.VMEM((C, C), BF16),
        pltpu.VMEM((3, C, C), BF16),
        pltpu.VMEM((3, C, C), BF16),
        pltpu.SemaphoreType.DMA((11,)),
        pltpu.VMEM((k0, PTS), BF16),
        pltpu.VMEM((k1, PTS), BF16),
        pltpu.VMEM((C, PTS), BF16),
        pltpu.VMEM((4, BLK, C), F32),
        pltpu.VMEM((4, BLK, C), F32),
        pltpu.VMEM((PTS, C), BF16),
        blocks,
        blocks,
        blocks,
        blocks,
        blocks,
        blocks,
        pltpu.VMEM((size_y, 1, PTS), jnp.int32),
        pltpu.VMEM((k0, C), BF16),
        pltpu.VMEM((size_y, OWN0, C), BF16),
        pltpu.VMEM((k0, C), BF16),
        pltpu.VMEM((size_y, OWN0, C), BF16),
        pltpu.VMEM((k1, 2 * C), BF16),
        pltpu.VMEM((size_q, 16, 2 * C), BF16),
        pltpu.VMEM((4, 16, 2 * C), BF16),
        pltpu.VMEM((size_z // 4, 16, 2 * C), BF16),
        pltpu.VMEM((k1, 2 * C), BF16),
        pltpu.VMEM((k1, C), BF16),
        pltpu.VMEM((size_q, 16, C), BF16),
        pltpu.VMEM((size_z, 16, C), BF16),
        pltpu.VMEM((k1, C), BF16),
        pltpu.VMEM((k0, 2 * C), BF16),
        pltpu.VMEM((C, k0), BF16),
        pltpu.VMEM((k0, (size_y + 2) // 3 * PTS), BF16),
        pltpu.VMEM((k1, size_y * PTS), BF16),
        pltpu.VMEM((k0, k1), F32),
        pltpu.VMEM((k0, k1), BF16),
        pltpu.VMEM((size_y, 16, C), BF16),
        pltpu.VMEM((size_q, 16, C), BF16),
        pltpu.VMEM((size_z, 16, C), BF16),
        pltpu.VMEM((size_y, 16, C), F32),
        pltpu.VMEM((size_y, 8, C), F32),
        pltpu.VMEM((8, C), F32),
        pltpu.VMEM((size_z, 8, C), F32),
        pltpu.SemaphoreType.DMA((17,)),
        pltpu.SemaphoreType.DMA((17,)),
        pltpu.SemaphoreType.DMA((8,)),
        pltpu.SemaphoreType.DMA((8,)),
        pltpu.SemaphoreType.DMA((size_y,)),
        pltpu.SemaphoreType.REGULAR,
    ]
    outs = pl.pallas_call(
        functools.partial(kernel, size_x, size_y),
        out_shape=(
            jax.ShapeDtypeStruct((PTS, C), BF16),
            jax.ShapeDtypeStruct((PTS, C), BF16),
            jax.ShapeDtypeStruct((7, C, C), F32),
        ),
        in_specs=[hbm] * 11,
        out_specs=(hbm,) * 3,
        scratch_shapes=scratch,
        name="layer",
        compiler_params=pltpu.CompilerParams(
            collective_id=0, has_side_effects=True, vmem_limit_bytes=60 * 1024 * 1024
        ),
    )(
        points.reshape(4, BLK, C),
        cotangent,
        local_tiles,
        local_source,
        halo_tiles.reshape(8, BLK, BLK),
        cluster_fine.reshape(1, PTS),
        cluster_mid.reshape(1, PTS),
        cluster_coarse.reshape(1, PTS),
        near_weight,
        up_weights,
        down_weights,
    )
    return pl.pallas_call(
        store,
        out_shape=tuple(jax.ShapeDtypeStruct(o.shape, o.dtype) for o in outs),
        in_specs=[hbm] * 3,
        out_specs=(hbm,) * 3,
        scratch_shapes=[pltpu.VMEM(o.shape, o.dtype) for o in outs] + [pltpu.SemaphoreType.DMA((2, 15))],
        name="store",
        compiler_params=pltpu.CompilerParams(vmem_limit_bytes=60 * 1024 * 1024),
    )(*outs)


def solution(mesh):
    rows = P(("gx", "gy"), None)
    flat = P(("gx", "gy"))
    size_x, size_y = mesh.shape["gx"], mesh.shape["gy"]
    return jax.shard_map(
        functools.partial(on_device, size_x, size_y),
        mesh=mesh,
        in_specs=(rows, rows, rows, rows, rows, flat, flat, flat, P(), P(), P()),
        out_specs=(rows, rows, P()),
        check_vma=False,
    )
```

```python
import functools
import math

import jax
import jax.numpy as jnp
from jax import lax
from jax.experimental import pallas as pl
from jax.experimental.pallas import tpu as pltpu
from jax.sharding import PartitionSpec as P

BLK = 128
C = 128
PTS = 512
OWN0 = 32
EPSILON = 1e-05
MESH = pl.DeviceIdType.MESH
F32, BF16 = jnp.float32, jnp.bfloat16

NN = ((1,), (0,))
NT = ((1,), (1,))
TN = ((0,), (0,))


def dot(a, b, dims=NN):
    return lax.dot_general(a, b, (dims, ((), ())), preferred_element_type=F32)


def dot_split(a, b, dims=NN):
    high = a.astype(BF16)
    low = (a - high.astype(F32)).astype(BF16)
    (left,), (right,) = dims
    return dot(
        jnp.concatenate([high, low], axis=left), jnp.concatenate([b, b], axis=right), dims
    )


def one_hot_rows(ids, first, count):
    rows = lax.broadcasted_iota(jnp.int32, (count, ids.shape[1]), 0) + first
    return jnp.where(rows == ids, 1.0, 0.0).astype(BF16)


def inverse_rms(summed):
    return lax.rsqrt(jnp.mean(summed * summed, axis=-1, keepdims=True) + EPSILON)


def norm_back(raw, normed, inverse):
    return inverse * (raw - normed * jnp.mean(raw * normed, axis=-1, keepdims=True))


def kernel(
    size_x,
    size_y,
    pts_in,
    cot_in,
    tiles_in,
    src_in,
    halo_in,
    c0_in,
    c1_in,
    c2_in,
    nw_in,
    up_in,
    dn_in,
    mixed_out,
    pg_out,
    wg_out,
    mixed_ref,
    pg_ref,
    wg_ref,
    out_sem,
    pts_ref,
    cot_ref,
    tiles_ref,
    src_ref,
    halo_ref,
    c0_ref,
    c1_ref,
    c2_ref,
    nw_ref,
    up_ref,
    dn_ref,
    load_sem,
    ot0,
    ot1,
    ot2,
    near,
    ret,
    nv,
    spx,
    spy,
    fx,
    fy,
    bx,
    by,
    ids,
    s_u0,
    r_u0,
    s_t0,
    r_t0,
    s_p1,
    r_p1,
    n_p1,
    f_p1,
    p1,
    s_u1,
    r_u1,
    z_u1,
    u1,
    ut0,
    u0_t,
    cat0,
    cat1,
    group,
    group_bf,
    s_p2,
    r_p2,
    z_p2,
    g_p2,
    s_d,
    r_d,
    z_d,
    send_sem,
    recv_sem,
    halo_send,
    halo_recv,
    ids_recv,
    relay,
):
    size_z = size_x // 2
    size_q = 2 * size_y
    k1 = size_x * size_y
    k2 = k1 // 8
    a = lax.axis_index("gx")
    b = lax.axis_index("gy")
    z = lax.div(a, 2)
    core = lax.rem(a, 2)
    q = core * size_y + b
    scale = 1.0 / math.sqrt(PTS * size_x * size_y)

    side_y = math.isqrt(size_y)
    side_x = size_y // side_y

    def in_plane(o):
        x = lax.rem(lax.div(b, side_x) + lax.div(o, side_x), side_y)
        return x * side_x + lax.rem(lax.rem(b, side_x) + lax.rem(o, side_x), side_x)

    def peer(kind, o):
        if kind == "y":
            i = in_plane(o)
            return i, (a, i)
        if kind == "z":
            i = lax.rem(z + o, size_z)
            return i, (i * 2 + core, b)
        if kind == "near":
            i = lax.rem(z + o, 4)
            return i, ((z - lax.rem(z, 4) + i) * 2 + core, b)
        if kind == "far":
            i = lax.rem(z + 4 * o, size_z)
            return lax.div(i, 4), (i * 2 + core, b)
        c = lax.rem(core + o, 2)
        i = in_plane(lax.div(o, 2))
        return c * size_y + i, (z * 2 + c, i)

    farthest = {
        "y": size_y // 2 + side_x // 2,
        "z": size_z // 2,
        "q": size_y + 2 * (side_x // 2),
        "near": 2,
        "far": size_z // 8,
    }
    count = {"y": size_y, "z": size_z, "q": size_q, "near": 4, "far": size_z // 4}

    def exchange(kind, step, source, target, landed=None):
        late = count[kind] - farthest[kind]

        def body(k, carry):
            i, device = peer(kind, jnp.where(k < late, k + farthest[kind], k - late + 1))
            pltpu.make_async_remote_copy(
                src_ref=source(i),
                dst_ref=target,
                send_sem=send_sem.at[step],
                recv_sem=recv_sem.at[step] if landed is None else landed,
                device_id=device,
                device_id_type=MESH,
            ).start()
            return carry

        lax.fori_loop(0, count[kind] - 1, body, 0)

    def arrived(step, ref):
        pltpu.make_async_copy(ref, ref, recv_sem.at[step]).wait()

    def id_arrived(i):
        pltpu.make_async_copy(ids.at[i], ids.at[i], ids_recv.at[i]).wait()

    def sent(step, ref):
        pltpu.make_async_copy(ref, ref, send_sem.at[step]).wait()

    loads = {
        name: pltpu.make_async_copy(source, target, load_sem.at[i])
        for i, (name, source, target) in enumerate(
            (
                ("c0", c0_in, c0_ref),
                ("pts", pts_in, pts_ref),
                ("cot", cot_in, cot_ref),
                ("c1", c1_in, c1_ref),
                ("c2", c2_in, c2_ref),
                ("nw", nw_in, nw_ref),
                ("src", src_in, src_ref),
                ("tiles", tiles_in, tiles_ref),
                ("halo", halo_in, halo_ref),
                ("up", up_in, up_ref),
                ("dn", dn_in, dn_ref),
            )
        )
    }
    barrier = pltpu.get_barrier_semaphore()

    reach = size_z // 4

    def greet(kind, steps, shift):
        def body(o, carry):
            _, device = peer(kind, o + shift)
            pl.semaphore_signal(barrier, inc=1, device_id=device, device_id_type=MESH)
            return carry

        lax.fori_loop(1, steps + 1, body, 0)

    far_q = farthest["q"]
    greet("q", size_q - far_q, far_q - 1)
    greet("q", far_q - 1, 0)
    greet("z", reach, 0)
    greet("z", reach, size_z - reach - 1)
    beside = lax.rem(a + size_x - 1 + 2 * core, size_x)
    pl.semaphore_signal(barrier, inc=1, device_id=(beside, b), device_id_type=MESH)

    for load in loads.values():
        load.start()

    for name in ("c0", "pts", "cot", "c1", "c2"):
        loads[name].wait()
    points = pts_ref[...].reshape(PTS, C)
    cot = cot_ref[...]
    c0, c1, c2 = c0_ref[...], c1_ref[...], c2_ref[...]
    ot0[...] = one_hot_rows(c0, 0, OWN0 * size_y)
    ot1[...] = one_hot_rows(c1, 0, k1)
    ot2[...] = one_hot_rows(c2, 0, C)
    both = dot(ot0[...], jnp.concatenate([points, cot], axis=1))
    s_u0[...] = both[:, :C].astype(BF16)
    s_t0[...] = both[:, C:].astype(BF16)
    ids[b] = c0 * 1024 + c1
    lane = lax.broadcasted_iota(jnp.int32, (k2, C), 1)
    t2 = dot(ot2[...], cot)[:k2]
    s_p1[:, :C] = dot(ot1[...], cot).astype(BF16)
    counts = dot(ot1[...], ot2[...], NT)
    s_p1[2 * k2 :, C:] = counts[2 * k2 :].astype(BF16)
    s_p1[:k2, C:] = jnp.where(lane < k2, counts[:k2], pltpu.roll(t2, C - k2, 1)).astype(BF16)
    s_p1[k2 : 2 * k2, C:] = jnp.where(lane < k2, counts[k2 : 2 * k2], t2).astype(BF16)

    for name in ("nw", "src", "tiles", "halo", "up", "dn"):
        loads[name].wait()
    near_grad = dot(cot, nw_ref[...], NT).astype(BF16)
    returned = [jnp.zeros((BLK, C), F32)] * 4
    for t in range(4):
        rows = slice(t * BLK, (t + 1) * BLK)
        tile = tiles_ref[rows, :]
        sources = jnp.concatenate([pts_ref[src_ref[t, k]] for k in range(3)], axis=0)
        near[t] = dot(tile, sources)
        grad = near_grad[rows]
        pieces = dot(tile, grad, TN)
        for k in range(3):
            piece = pieces[k * BLK : (k + 1) * BLK]
            for s in range(4):
                returned[s] = returned[s] + jnp.where(src_ref[t, k] == s, piece, 0.0)
        spx[t] = dot(halo_ref[2 * t], grad, TN).astype(BF16)
        spy[t] = dot(halo_ref[2 * t + 1], grad, TN).astype(BF16)
    for s in range(4):
        ret[s] = returned[s]

    pl.semaphore_wait(barrier, 2 * reach + size_q - 1 + 1)
    for o in (reach, size_z - reach):
        _, device = peer("z", o)
        pl.semaphore_signal(relay, inc=1, device_id=device, device_id_type=MESH)

    exchange("y", 0, lambda i: ids.at[b], ids.at[b], ids_recv.at[b])
    exchange("y", 1, lambda i: s_u0.at[pl.ds(i * OWN0, OWN0)], r_u0.at[b])
    exchange("q", 2, lambda i: s_p1.at[pl.ds(i * 16, 16)], r_p1.at[q])
    has = (a > 0, a < size_x - 1, b > 0, b < size_y - 1)

    def halo_copies(side):
        if side == 0:
            return [[(pts_ref.at[pl.ds(0, 2)], fx.at[pl.ds(2, 2)])], [(spx.at[pl.ds(0, 2)], bx.at[pl.ds(2, 2)])]]
        if side == 1:
            return [[(pts_ref.at[pl.ds(2, 2)], fx.at[pl.ds(0, 2)])], [(spx.at[pl.ds(2, 2)], bx.at[pl.ds(0, 2)])]]
        if side == 2:
            return [[(pts_ref.at[i], fy.at[i + 1]) for i in (0, 2)], [(spy.at[i], by.at[i + 1]) for i in (0, 2)]]
        return [[(pts_ref.at[i], fy.at[i - 1]) for i in (1, 3)], [(spy.at[i], by.at[i - 1]) for i in (1, 3)]]

    neighbour = ((a - 1, b), (a + 1, b), (a, b - 1), (a, b + 1))
    landing = ((fx, bx, 0, 2), (fx, bx, 2, 4), (fy, by, 0, 2), (fy, by, 2, 4))
    edge = ((0, 1), (2, 3), (0, 2), (1, 3))

    def send_halo(kind, sides):
        for side in sides:

            @pl.when(has[side])
            def _(side=side):
                for source, target in halo_copies(side)[kind]:
                    pltpu.make_async_remote_copy(
                        src_ref=source,
                        dst_ref=target,
                        send_sem=halo_send.at[2 * side + kind],
                        recv_sem=halo_recv.at[2 * (side ^ 1) + kind],
                        device_id=neighbour[side],
                        device_id_type=MESH,
                    ).start()

    def wait_halo(kind):
        for side in range(4):
            ref = landing[side][kind]

            @pl.when(has[side])
            def _(side=side, ref=ref):
                two = ref.at[pl.ds(landing[side][2], 2)]
                pltpu.make_async_copy(two, two, halo_recv.at[2 * side + kind]).wait()

            @pl.when(jnp.logical_not(has[side]))
            def _(side=side, ref=ref):
                for i in edge[side]:
                    ref[i] = jnp.zeros((BLK, C), BF16)

    send_halo(0, (0, 1))
    send_halo(1, (0, 1))

    near_first = sorted(
        range(size_y),
        key=lambda o: min(o // side_x, side_y - o // side_x) + min(o % side_x, side_x - o % side_x),
    )
    fines = []
    pair_counts = jnp.zeros((OWN0, k1), F32)
    for n, o in enumerate(near_first):
        i = in_plane(o)
        if n > 0:
            id_arrived(i)
        packed = ids[i]
        fine = lax.shift_right_logical(packed, 10)
        mid = lax.bitwise_and(packed, 1023)
        fines.append(fine)
        here = slice(n * PTS, (n + 1) * PTS)
        cat1[:, here] = one_hot_rows(mid, 0, k1)
        pair_counts = pair_counts + dot(one_hot_rows(fine, b * OWN0, OWN0), cat1[:, here], NT)
    pair_counts = pair_counts.astype(BF16)

    def group_counts(first, last):
        for n in range(first, last):
            cat0[:, (n - first) * PTS : (n - first + 1) * PTS] = one_hot_rows(fines[n], 0, OWN0 * size_y)
        part = dot(cat0[:, : (last - first) * PTS], cat1[:, first * PTS : last * PTS], NT)
        if first == 0:
            group[...] = part
        else:
            group[...] += part

    r_u0[b] = s_u0[pl.ds(pl.multiple_of(b * OWN0, OWN0), OWN0), :]
    arrived(1, r_u0.at[pl.ds(0, size_y - 1)])
    u0 = jnp.sum(r_u0[...].astype(F32), axis=0)
    summed0 = dot_split(u0, up_ref[0])
    inverse0 = inverse_rms(summed0)
    normed0 = summed0 * inverse0
    n0 = normed0.astype(BF16)
    s_u1[...] = dot(pair_counts, n0, TN).astype(BF16)
    exchange("q", 4, lambda i: s_u1.at[pl.ds(i * 16, 16)], r_u1.at[q])
    mine32 = pl.ds(pl.multiple_of(b * OWN0, OWN0), OWN0)
    exchange("y", 3, lambda i: s_t0.at[pl.ds(i * OWN0, OWN0)], r_t0.at[b])

    mine16 = pl.ds(pl.multiple_of(q * 16, 16), 16)
    r_p1[q] = s_p1[mine16, :]
    arrived(2, r_p1.at[pl.ds(0, size_q - 1)])
    z_near, z_far = lax.rem(z, 4), lax.div(z, 4)
    n_p1[z_near] = jnp.sum(r_p1[...].astype(F32), axis=0).astype(BF16)
    pl.semaphore_wait(relay, 2)
    exchange("near", 6, lambda i: n_p1.at[z_near], n_p1.at[z_near])

    third = (size_y + 2) // 3
    group_counts(0, third)

    arrived(6, n_p1.at[pl.ds(0, 3)])
    f_p1[z_far] = jnp.sum(n_p1[...].astype(F32), axis=0).astype(BF16)
    exchange("far", 14, lambda i: f_p1.at[z_far], f_p1.at[z_far])

    r_u1[q] = s_u1[mine16, :]
    arrived(4, r_u1.at[pl.ds(0, size_q - 1)])
    z_u1[z] = jnp.sum(r_u1[...].astype(F32), axis=0).astype(BF16)
    exchange("z", 8, lambda i: z_u1.at[z], z_u1.at[z])

    r_t0[b] = s_t0[mine32, :]
    arrived(3, r_t0.at[pl.ds(0, size_y - 1)])
    t0 = jnp.sum(r_t0[...].astype(F32), axis=0)
    ut0[mine32, :C] = u0.astype(BF16)
    ut0[mine32, C:] = t0.astype(BF16)
    exchange("y", 5, lambda i: ut0.at[mine32], ut0.at[mine32])
    send_halo(0, (2, 3))
    group_counts(third, 2 * third)

    wait_halo(0)
    for t in range(4):
        total = near[t] + dot(halo_ref[2 * t], fx[t]) + dot(halo_ref[2 * t + 1], fy[t])
        nv[pl.ds(t * BLK, BLK), :] = total.astype(BF16)
    near_part = dot(nv[...], cot, TN)
    down0_part = dot(n0, t0.astype(BF16), TN)
    s_p2[...] = jnp.concatenate(
        [near_part.reshape(size_y, 8, C), down0_part.reshape(size_y, 8, C)], axis=1
    ).astype(BF16)
    exchange("q", 7, lambda i: s_p2.at[lax.rem(i, size_y)], r_p2.at[q])

    arrived(5, ut0.at[pl.ds(0, (size_y - 1) * OWN0)])
    u0_t[...] = ut0[:, :C].astype(F32).T.astype(BF16)
    summed0 = dot(ut0[:, :C], up_ref[0])
    inverse0 = inverse_rms(summed0)
    normed0 = summed0 * inverse0
    raw0 = dot(ut0[:, C:], dn_ref[0], NT)

    arrived(14, f_p1.at[pl.ds(0, size_z // 4 - 1)])
    p1[mine16, :] = jnp.sum(f_p1[...].astype(F32), axis=0).astype(BF16)
    exchange("q", 9, lambda i: p1.at[mine16], p1.at[mine16])

    arrived(8, z_u1.at[pl.ds(0, size_z - 1)])
    u1[mine16, :] = jnp.sum(z_u1[...].astype(F32), axis=0).astype(BF16)
    exchange("q", 11, lambda i: u1.at[mine16], u1.at[mine16])

    group_counts(2 * third, size_y)
    group_bf[...] = group[...].astype(BF16)
    combined = points.astype(F32) + dot(nv[...], nw_ref[...])
    combined = combined + dot(dot(ot0[...], normed0.astype(BF16), TN).astype(BF16), dn_ref[0])
    arrived(9, p1.at[pl.ds(0, (size_q - 1) * 16)])
    t1 = p1[:, :C]
    upper_part = p1[:k2, C:].astype(F32)
    t2 = jnp.where(lane < k2, pltpu.roll(upper_part, C - k2, 1), p1[k2 : 2 * k2, C:].astype(F32))
    t2 = t2.astype(BF16)
    counts = p1[:, C:][:, :k2]
    counts_t = counts.astype(F32).T.astype(BF16)
    wide = p1[:, C:].astype(F32)
    half = lax.broadcasted_iota(jnp.int32, (k1, C), 1) < k2
    counts_twice = jnp.where(half, wide, pltpu.roll(wide, k2, 1)).astype(BF16)

    r_p2[q] = s_p2[b]
    arrived(7, r_p2.at[pl.ds(0, size_q - 1)])
    z_p2[z] = jnp.sum(r_p2[...].astype(F32), axis=0).astype(BF16)
    exchange("z", 10, lambda i: z_p2.at[z], z_p2.at[z])

    raw2 = dot(t2, dn_ref[2], NT)
    raw1 = dot(t1, dn_ref[1], NT)
    arrived(11, u1.at[pl.ds(0, (size_q - 1) * 16)])
    summed1 = dot(u1[...], up_ref[1])
    inverse1 = inverse_rms(summed1)
    normed1 = summed1 * inverse1
    n1 = normed1.astype(BF16)
    u2 = dot(counts_t, n1)
    summed2 = dot_split(u2, up_ref[2])
    inverse2 = inverse_rms(summed2)
    normed2 = summed2 * inverse2
    n2 = normed2.astype(BF16)
    sg2 = norm_back(raw2, normed2, inverse2).astype(BF16)
    back2 = dot(sg2, up_ref[2], NT)
    back2_high = back2.astype(BF16)
    back2_low = (back2 - back2_high.astype(F32)).astype(BF16)
    raw1 = raw1 + dot(counts_twice, jnp.concatenate([back2_high, back2_low], axis=0))
    sg1 = norm_back(raw1, normed1, inverse1).astype(BF16)
    raw0 = raw0 + dot_split(dot(group_bf[...], sg1), up_ref[1], NT)
    sg0 = norm_back(raw0, normed0, inverse0).astype(BF16)
    s_d[...] = dot(u0_t[...], sg0).reshape(size_y, 8, C)
    to_pair = pltpu.make_async_remote_copy(
        src_ref=s_d.at[b],
        dst_ref=r_d,
        send_sem=send_sem.at[13],
        recv_sem=recv_sem.at[13],
        device_id=(a + 1 - 2 * core, b),
        device_id_type=MESH,
    )
    to_pair.start()

    wg_ref[2] = dot(u1[...], sg1, TN) * scale
    wg_ref[3] = dot_split(u2, sg2, TN) * scale
    to_pair.wait()
    z_d[z] = s_d[b] + r_d[...]
    exchange("z", 15, lambda i: z_d.at[z], z_d.at[z])
    send_halo(1, (2, 3))
    wg_ref[5] = dot(n1, t1, TN) * scale
    wg_ref[6] = dot(n2, t2, TN) * scale

    arrived(10, z_p2.at[pl.ds(0, size_z - 1)])
    g_p2[b] = jnp.sum(z_p2[...].astype(F32), axis=0) * scale
    exchange("y", 12, lambda i: g_p2.at[b], g_p2.at[b])

    combined = combined + dot(dot(ot1[...], n1, TN).astype(BF16), dn_ref[1])
    combined = combined + dot(dot(ot2[:k2, :], n2, TN).astype(BF16), dn_ref[2])
    mixed_ref[...] = combined.astype(BF16)
    put_mixed = pltpu.make_async_copy(mixed_ref, mixed_out, out_sem.at[0])
    put_mixed.start()

    wait_halo(1)
    for t in range(4):
        ret[t] = ret[t] + bx[t].astype(F32) + by[t].astype(F32)
    upper0 = dot(ot0[...], sg0, TN).astype(BF16)
    grad = cot.astype(F32) + ret[...].reshape(PTS, C) + dot(upper0, up_ref[0], NT)
    pg_ref[...] = grad.astype(BF16)
    put_pg = pltpu.make_async_copy(pg_ref, pg_out, out_sem.at[1])
    put_pg.start()

    arrived(12, g_p2.at[pl.ds(0, size_y - 1)])
    wg_ref[0] = g_p2[:, :8, :].reshape(C, C)
    wg_ref[4] = g_p2[:, 8:, :].reshape(C, C)
    put_first = pltpu.make_async_copy(wg_ref.at[0], wg_out.at[0], out_sem.at[2])
    put_first.start()
    put_rest = pltpu.make_async_copy(wg_ref.at[pl.ds(2, 5)], wg_out.at[pl.ds(2, 5)], out_sem.at[3])
    put_rest.start()

    arrived(15, z_d.at[pl.ds(0, size_z - 1)])
    mine8 = pl.ds(pl.multiple_of(b * 8, 8), 8)
    wg_ref[1, mine8, :] = jnp.sum(z_d[...], axis=0) * scale
    exchange("y", 16, lambda i: wg_ref.at[1, mine8], wg_out.at[1, mine8])
    put_last = pltpu.make_async_copy(wg_ref.at[1, mine8], wg_out.at[1, mine8], out_sem.at[4])
    put_last.start()
    for step, ref in (
        (0, ids.at[pl.ds(0, size_y - 1)]),
        (1, r_u0.at[pl.ds(0, size_y - 1)]),
        (2, r_p1.at[pl.ds(0, size_q - 1)]),
        (3, r_t0.at[pl.ds(0, size_y - 1)]),
        (4, r_u1.at[pl.ds(0, size_q - 1)]),
        (5, ut0.at[pl.ds(0, (size_y - 1) * OWN0)]),
        (6, n_p1.at[pl.ds(0, 3)]),
        (14, f_p1.at[pl.ds(0, size_z // 4 - 1)]),
        (7, r_p2.at[pl.ds(0, size_q - 1)]),
        (8, z_u1.at[pl.ds(0, size_z - 1)]),
        (9, p1.at[pl.ds(0, (size_q - 1) * 16)]),
        (10, z_p2.at[pl.ds(0, size_z - 1)]),
        (11, u1.at[pl.ds(0, (size_q - 1) * 16)]),
        (12, g_p2.at[pl.ds(0, size_y - 1)]),
        (15, z_d.at[pl.ds(0, size_z - 1)]),
    ):
        sent(step, ref)
    for side in range(4):

        @pl.when(has[side])
        def _(side=side):
            for kind in range(2):
                two = fx.at[pl.ds(0, 2)]
                pltpu.make_async_copy(two, two, halo_send.at[2 * side + kind]).wait()

    for put in (put_mixed, put_pg, put_first, put_rest, put_last):
        put.wait()
    arrived(16, wg_out.at[1, pl.ds(0, (size_y - 1) * 8)])
    sent(16, wg_out.at[1, pl.ds(0, (size_y - 1) * 8)])


def store(*refs):
    sources, targets, held, sem = refs[:3], refs[3:6], refs[6:9], refs[9]
    parts = [(2, pl.ds(i, 1)) for i in range(7)]
    parts += [(n, pl.ds(i * BLK, BLK)) for n in (0, 1) for i in range(PTS // BLK)]
    first, then = [], []
    for p, (n, part) in enumerate(parts):
        first.append(pltpu.make_async_copy(sources[n].at[part], held[n].at[part], sem.at[0, p]))
        then.append(pltpu.make_async_copy(held[n].at[part], targets[n].at[part], sem.at[1, p]))
    for copy in first:
        copy.start()
    for p in range(len(parts)):
        first[p].wait()
        then[p].start()
    for copy in then:
        copy.wait()


def on_device(
    size_x,
    size_y,
    points,
    cotangent,
    local_tiles,
    local_source,
    halo_tiles,
    cluster_fine,
    cluster_mid,
    cluster_coarse,
    near_weight,
    up_weights,
    down_weights,
):
    size_z, size_q, k1 = size_x // 2, 2 * size_y, size_x * size_y
    k0 = OWN0 * size_y
    blocks = pltpu.VMEM((4, BLK, C), BF16)
    hbm = pl.BlockSpec(memory_space=pltpu.HBM)
    scratch = [
        pltpu.VMEM((PTS, C), BF16),
        pltpu.VMEM((PTS, C), BF16),
        pltpu.VMEM((7, C, C), F32),
        pltpu.SemaphoreType.DMA((5,)),
        pltpu.VMEM((4, BLK, C), BF16),
        pltpu.VMEM((PTS, C), BF16),
        pltpu.VMEM((PTS, 3 * BLK), BF16),
        pltpu.SMEM((4, 3), jnp.int32),
        pltpu.VMEM((8, BLK, BLK), BF16),
        pltpu.VMEM((1, PTS), jnp.int32),
        pltpu.VMEM((1, PTS), jnp.int32),
        pltpu.VMEM((1, PTS), jnp.int32),
        pltpu.VMEM((C, C), BF16),
        pltpu.VMEM((3, C, C), BF16),
        pltpu.VMEM((3, C, C), BF16),
        pltpu.SemaphoreType.DMA((11,)),
        pltpu.VMEM((k0, PTS), BF16),
        pltpu.VMEM((k1, PTS), BF16),
        pltpu.VMEM((C, PTS), BF16),
        pltpu.VMEM((4, BLK, C), F32),
        pltpu.VMEM((4, BLK, C), F32),
        pltpu.VMEM((PTS, C), BF16),
        blocks,
        blocks,
        blocks,
        blocks,
        blocks,
        blocks,
        pltpu.VMEM((size_y, 1, PTS), jnp.int32),
        pltpu.VMEM((k0, C), BF16),
        pltpu.VMEM((size_y, OWN0, C), BF16),
        pltpu.VMEM((k0, C), BF16),
        pltpu.VMEM((size_y, OWN0, C), BF16),
        pltpu.VMEM((k1, 2 * C), BF16),
        pltpu.VMEM((size_q, 16, 2 * C), BF16),
        pltpu.VMEM((4, 16, 2 * C), BF16),
        pltpu.VMEM((size_z // 4, 16, 2 * C), BF16),
        pltpu.VMEM((k1, 2 * C), BF16),
        pltpu.VMEM((k1, C), BF16),
        pltpu.VMEM((size_q, 16, C), BF16),
        pltpu.VMEM((size_z, 16, C), BF16),
        pltpu.VMEM((k1, C), BF16),
        pltpu.VMEM((k0, 2 * C), BF16),
        pltpu.VMEM((C, k0), BF16),
        pltpu.VMEM((k0, (size_y + 2) // 3 * PTS), BF16),
        pltpu.VMEM((k1, size_y * PTS), BF16),
        pltpu.VMEM((k0, k1), F32),
        pltpu.VMEM((k0, k1), BF16),
        pltpu.VMEM((size_y, 16, C), BF16),
        pltpu.VMEM((size_q, 16, C), BF16),
        pltpu.VMEM((size_z, 16, C), BF16),
        pltpu.VMEM((size_y, 16, C), F32),
        pltpu.VMEM((size_y, 8, C), F32),
        pltpu.VMEM((8, C), F32),
        pltpu.VMEM((size_z, 8, C), F32),
        pltpu.SemaphoreType.DMA((17,)),
        pltpu.SemaphoreType.DMA((17,)),
        pltpu.SemaphoreType.DMA((8,)),
        pltpu.SemaphoreType.DMA((8,)),
        pltpu.SemaphoreType.DMA((size_y,)),
        pltpu.SemaphoreType.REGULAR,
    ]
    outs = pl.pallas_call(
        functools.partial(kernel, size_x, size_y),
        out_shape=(
            jax.ShapeDtypeStruct((PTS, C), BF16),
            jax.ShapeDtypeStruct((PTS, C), BF16),
            jax.ShapeDtypeStruct((7, C, C), F32),
        ),
        in_specs=[hbm] * 11,
        out_specs=(hbm,) * 3,
        scratch_shapes=scratch,
        name="layer",
        compiler_params=pltpu.CompilerParams(
            collective_id=0, has_side_effects=True, vmem_limit_bytes=60 * 1024 * 1024
        ),
    )(
        points.reshape(4, BLK, C),
        cotangent,
        local_tiles,
        local_source,
        halo_tiles.reshape(8, BLK, BLK),
        cluster_fine.reshape(1, PTS),
        cluster_mid.reshape(1, PTS),
        cluster_coarse.reshape(1, PTS),
        near_weight,
        up_weights,
        down_weights,
    )
    return pl.pallas_call(
        store,
        out_shape=tuple(jax.ShapeDtypeStruct(o.shape, o.dtype) for o in outs),
        in_specs=[hbm] * 3,
        out_specs=(hbm,) * 3,
        scratch_shapes=[pltpu.VMEM(o.shape, o.dtype) for o in outs] + [pltpu.SemaphoreType.DMA((2, 15))],
        name="store",
        compiler_params=pltpu.CompilerParams(vmem_limit_bytes=60 * 1024 * 1024),
    )(*outs)


def solution(mesh):
    rows = P(("gx", "gy"), None)
    flat = P(("gx", "gy"))
    size_x, size_y = mesh.shape["gx"], mesh.shape["gy"]
    return jax.shard_map(
        functools.partial(on_device, size_x, size_y),
        mesh=mesh,
        in_specs=(rows, rows, rows, rows, rows, flat, flat, flat, P(), P(), P()),
        out_specs=(rows, rows, P()),
        check_vma=False,
    )
```
